128 devices in a mesh: grp: 16 (over z, x), tp: 8 (over y, core).
Axes of the slice: x: 4, y: 4, z: 4, core: 2. Of those that a mesh axis runs over, the one named last changes fastest.
Arguments:
- queries: bfloat16 [128, 48, 128], P('grp', 'tp'), may hold values from -32 to 32
- kv_cache: bfloat16 [128, 2, 8, 384, 128], P('grp', None, 'tp'), may hold values from -6 to 6
- new_kv: bfloat16 [128, 2, 8, 128], P('grp', None, 'tp'), may hold values from -6 to 6
- lengths: int32 [128], P('grp'), may hold values from 1 to 383, as said below
- residual: bfloat16 [128, 6144], P('grp', 'tp'), may hold values from -9 to 9
- w_out: bfloat16 [6144, 6144], P('tp'), may hold values from -0.078125 to 0.078125
- norm_gain: bfloat16 [6144], P('tp'), may hold values from 0.099609375 to 1.8984375
- expert_ids: int32 [128, 2], P('grp'), may hold values from 0 to 3, all different within a row; in each aligned block of 8 rows (0 to 7, 8 to 15, ...) at most 8 rows name the same one
- gate_w: float32 [128, 2], P('grp'), may hold values from 0.25 to 1
- w_inner: bfloat16 [6144, 2, 32768], P(None, None, ('grp', 'tp')), may hold values from -0.078125 to 0.078125
- w_down: bfloat16 [32768, 6144], P(('grp', 'tp')), may hold values from -0.0625 to 0.0625
- mig_rows: int32 [8], replicated, may hold values from 0 to 127, as said below
- mig_dest: int32 [8], replicated, may hold values from 0 to 15, as said below
Outputs:
- mixed: bfloat16 [128, 6144], P('grp', 'tp')
- landed: bfloat16 [16, 2, 8, 384, 128], P('grp', None, 'tp')
The draws below stay inside these ranges and needn't reach their ends.
Inputs may be any that keep to these rules, and one draw needn't show every extreme that they name: `lengths`: the longest cache holds 383 tokens, so the new token always has a free position. `expert_ids`: each row names two different experts. `mig_rows`: the listed rows lie in distinct replicas. `mig_dest`: the destinations are distinct, and none is the replica that holds the row at the same position of the list.
All inputs are finite; a program needn't handle non-finite values.
Results may differ from the reference program's by a relative error of at most 0.012.
Values may be sent and summed in bfloat16 or wider, within the bound.
A program may use at most 128 MiB of HBM per device.

```python
import math
import jax
import jax.numpy as jnp
import numpy as np
from jax import lax

D = 6144
HEADS = 48
KVH = 8
HD = 128
FF = 8192
EXPERTS = 4
MIG = 8
CACHE = 384
ROWS_REP = 8
REPLICAS = 16
TOKENS = 128


def migration(key):
    order = jax.random.permutation(jax.random.fold_in(key, 21), TOKENS // ROWS_REP)
    sources = order[:MIG]
    offsets = jax.random.randint(jax.random.fold_in(key, 22), (MIG,), 0, ROWS_REP)
    return (sources * ROWS_REP + offsets, jnp.roll(sources, -1))


def draw_queries(key, part):
    key = jax.random.fold_in(key, 1)
    values = jnp.clip(jax.random.normal(key, (TOKENS, HEADS, HD)), -6.0, 6.0)
    return values.astype(jnp.bfloat16)


def draw_kv_cache(key, part):
    key = jax.random.fold_in(key, 2)
    shape_all = (TOKENS, 2, KVH, CACHE, HD)
    values = jnp.clip(jax.random.normal(key, shape_all), -6.0, 6.0)
    return values.astype(jnp.bfloat16)


def draw_new_kv(key, part):
    key = jax.random.fold_in(key, 3)
    shape_all = (TOKENS, 2, KVH, HD)
    values = jnp.clip(jax.random.normal(key, shape_all), -6.0, 6.0)
    return values.astype(jnp.bfloat16)


def draw_residual(key, part):
    key = jax.random.fold_in(key, 4)
    ramp = 0.5 * jnp.exp(jnp.log(3.0) * jnp.arange(D, dtype=jnp.float32) / D)
    values = jnp.clip(jax.random.normal(key, (TOKENS, D)), -6.0, 6.0) * ramp[None, :]
    return values.astype(jnp.bfloat16)


def draw_lengths(key, part):
    key = jax.random.fold_in(key, 5)
    replica_caps = jax.random.randint(jax.random.fold_in(key, 50), (TOKENS // ROWS_REP,), CACHE // 4, CACHE)
    raw_draw = jax.random.randint(jax.random.fold_in(key, 51), (TOKENS,), 0, CACHE)
    row_lengths = 1 + raw_draw % replica_caps[jnp.arange(TOKENS) // ROWS_REP]
    chosen_row = jax.random.randint(jax.random.fold_in(key, 52), (), 0, TOKENS)
    return jnp.where(jnp.arange(TOKENS) == chosen_row, CACHE - 1, row_lengths).astype(jnp.int32)


def draw_mig_rows(key, part):
    moved, targets = migration(key)
    return moved.astype(jnp.int32)


def draw_mig_dest(key, part):
    moved, targets = migration(key)
    return targets.astype(jnp.int32)


def levels(key, dims, shards, least, largest):
    level, own = 1.0, jax.random.fold_in(key, 6)
    for axis_at, shards_of in shards:
        steps = jnp.exp(jax.random.uniform(jax.random.fold_in(own, axis_at), (shards_of,), jnp.float32, least / len(shards), largest / len(shards)))
        level = level * jnp.repeat(steps, dims[axis_at] // shards_of).reshape([-1 if axis == axis_at else 1 for axis in range(len(dims))])
    return level


def deal_out(key, own, number, rows, number_of, top, bound, slope):
    ranking = jax.random.permutation(key, number_of)
    crowded, common = portions_of(number_of, rows * top, bound, slope, True), portions_of(number_of, rows * top, bound, slope, False)
    places = jnp.arange(number_of)

    def named(sizes, turn):
        used = int((sizes > 0).sum())
        fixed = max(1, used // 4)
        shifted = fixed + (places - fixed + turn * (used - fixed)) % max(1, number_of - fixed)
        return jnp.zeros((number_of,), jnp.int32).at[ranking[jnp.where(places < fixed, places, shifted)]].set(jnp.asarray(sizes, jnp.int32))

    sizes = jnp.where(number % 4 == 0, named(crowded, number // 4), named(common, number - number // 4 - 1))
    mixed = jax.random.permutation(jax.random.fold_in(own, 3), number_of)
    source_of, receiver = mixed[0:number_of // 2 * 2:2], mixed[1:number_of // 2 * 2:2]
    room = jnp.minimum(sizes[source_of] - 1, bound - sizes[receiver]) // 2
    room = jnp.where((source_of == ranking[0]) | (receiver == ranking[0]) | (sizes[receiver] == 0), 0, jnp.maximum(room, 0))
    shifted = jax.random.randint(jax.random.fold_in(own, 4), (number_of // 2,), 0, 1 << 20) % (room + 1)
    sizes = sizes.at[source_of].add(-shifted).at[receiver].add(shifted)
    items = jnp.searchsorted(jnp.cumsum(sizes), jnp.arange(rows * top), side="right").astype(jnp.int32)
    table = items.reshape(top, rows).T
    table = table[jax.random.permutation(jax.random.fold_in(own, 1), rows)]
    turn = jax.random.randint(jax.random.fold_in(own, 2), (rows, 1), 0, top)
    return jnp.take_along_axis(table, (jnp.arange(top)[None, :] + turn) % top, axis=1)


def portions_of(amount, total, bound, lean, full):
    loads = [(1 << 20) // math.isqrt(standing ** lean) + 1 for standing in range(1, amount + 1)]
    largest = bound if full else min(bound, max(-(-total // amount), total * loads[0] // sum(loads)))
    least = 1 if total - largest >= amount - 1 else 0
    holding, surplus = [largest] + [least] * (amount - 1), total - largest - least * (amount - 1)
    while surplus > 0:
        free = [i for i in range(1, amount) if holding[i] < largest] or [i for i in range(1, amount) if holding[i] < bound]
        mass, budget = sum([loads[i] for i in free]), surplus
        for i in free:
            addition = min(bound - holding[i], max(1, budget * loads[i] // mass), surplus)
            holding[i] = holding[i] + addition
            surplus = surplus - addition
    return np.array(holding)


def normal_values(rng, extent, scale, reach, pieces=(), held_as=jnp.bfloat16):
    result = jax.random.normal(rng, extent, jnp.float32) * scale
    if len(pieces) > 0:
        result = levels(rng, extent, pieces, -0.22, 0.18) * result
    return jnp.clip(result, min=-reach, max=reach).astype(held_as)


def setup_inputs(seed: int = 0) -> dict:
    seeds = jax.random.split(jax.random.key(seed), 14)
    queries = draw_queries(jax.random.fold_in(seeds[13], 71), 0)
    kv_cache = draw_kv_cache(jax.random.fold_in(seeds[13], 71), 0)
    new_kv = draw_new_kv(jax.random.fold_in(seeds[13], 71), 0)
    lengths = draw_lengths(jax.random.fold_in(seeds[13], 71), 0)
    residual = draw_residual(jax.random.fold_in(seeds[13], 71), 0)
    w_out = normal_values(seeds[5], (HEADS * HD, D), (HEADS * HD) ** -0.5, 0.078125, ((0, 8),))
    norm_gain = jnp.clip(1.0 + 0.18 * jax.random.normal(seeds[6], (D,), jnp.float32), 0.099609375, 1.8984375).astype(jnp.bfloat16)
    expert_ids_keys = jax.random.split(jax.random.fold_in(seeds[7], 1), TOKENS // ROWS_REP)
    expert_ids_turns = jax.random.permutation(jax.random.fold_in(seeds[7], 3), TOKENS // ROWS_REP)
    expert_ids = jax.vmap(lambda own, number: deal_out(jax.random.fold_in(seeds[7], 2), own, number, ROWS_REP, EXPERTS, 2, ROWS_REP, 2))(expert_ids_keys, expert_ids_turns).reshape((TOKENS, 2))
    gate_w = jnp.clip(0.25 + 0.75 * jax.random.uniform(seeds[8], (TOKENS, 2), jnp.float32) ** levels(seeds[8], (TOKENS, 2), ((0, 16),), -0.2, 0.2), 0.25, 1.0)
    w_inner = normal_values(seeds[9], (D, 2, EXPERTS * FF), D ** -0.5, 0.078125, ((2, 128),))
    w_down = normal_values(seeds[10], (EXPERTS * FF, D), FF ** -0.5, 0.0625, ((0, 128),))
    mig_rows = draw_mig_rows(jax.random.fold_in(seeds[13], 71), 0)
    mig_dest = draw_mig_dest(jax.random.fold_in(seeds[13], 71), 0)
    return {"queries": queries, "kv_cache": kv_cache, "new_kv": new_kv, "lengths": lengths, "residual": residual, "w_out": w_out, "norm_gain": norm_gain, "expert_ids": expert_ids, "gate_w": gate_w, "w_inner": w_inner, "w_down": w_down, "mig_rows": mig_rows, "mig_dest": mig_dest}


def attend_group(queries, kv_block, fresh_kv, lengths):
    row_count, head_count, feature_dim = queries.shape
    kv_heads = kv_block.shape[2]
    span_len = kv_block.shape[3]
    grouped = queries.astype(jnp.float32).reshape(row_count, kv_heads, head_count // kv_heads, feature_dim)
    scaling = feature_dim ** (-0.5)
    scores = jnp.einsum('rkgd,rkpd->rkgp', grouped, kv_block[:, 0].astype(jnp.float32)) * scaling
    own_score = jnp.einsum('rkgd,rkd->rkg', grouped, fresh_kv[:, 0].astype(jnp.float32)) * scaling
    visible = (jnp.arange(span_len, dtype=jnp.int32)[None, :] < lengths[:, None])[:, None, None, :]
    masked = jnp.where(visible, scores, -jnp.inf)
    highest = jnp.maximum(lax.optimization_barrier(jnp.max(masked, axis=-1)), own_score)
    spread = jnp.where(visible, jnp.exp(masked - highest[..., None]), 0.0)
    own_exp = jnp.exp(own_score - highest)
    denominator = lax.optimization_barrier(jnp.sum(spread, axis=-1)) + own_exp
    weights = (spread / denominator[..., None]).astype(jnp.bfloat16)
    own_weight = (own_exp / denominator).astype(jnp.bfloat16)
    mixture = jnp.einsum('rkgp,rkpd->rkgd', weights.astype(jnp.float32), kv_block[:, 1].astype(jnp.float32))
    mixture = mixture + own_weight.astype(jnp.float32)[..., None] * fresh_kv[:, 1].astype(jnp.float32)[:, :, None, :]
    return mixture.astype(jnp.bfloat16).reshape(row_count, head_count * feature_dim)

def seal(kv_slab, fresh_kv, length):
    positions = jnp.arange(kv_slab.shape[-2], dtype=jnp.int32)[:, None]
    return jnp.where(positions < length, kv_slab, jnp.where(positions == length, fresh_kv[:, :, None, :], jnp.zeros_like(kv_slab)))

def reference(queries, kv_cache, new_kv, lengths, residual, w_out, norm_gain, expert_ids, gate_w, w_inner, w_down, mig_rows, mig_dest):
    group_size = HEADS // KVH
    outputs = []
    for head_pos in range(KVH):
        outputs.append(attend_group(queries[:, head_pos * group_size:(head_pos + 1) * group_size], kv_cache[:, :, head_pos:head_pos + 1], new_kv[:, :, head_pos:head_pos + 1], lengths))
    heads_out = jnp.concatenate(outputs, axis=1)
    hidden_state = residual.astype(jnp.float32) + jnp.dot(heads_out, w_out, preferred_element_type=jnp.float32)
    squares = lax.optimization_barrier(jnp.mean(hidden_state * hidden_state, axis=1))
    normed = (hidden_state * lax.rsqrt(squares + 1e-05)[:, None] * norm_gain.astype(jnp.float32)[None, :]).astype(jnp.bfloat16)
    moe_out = jnp.zeros(hidden_state.shape, jnp.float32)
    for expert in range(EXPERTS):
        gate_cols = w_inner[:, 0, expert * FF:(expert + 1) * FF]
        up_cols = w_inner[:, 1, expert * FF:(expert + 1) * FF]
        gate_part = jnp.dot(normed, gate_cols, preferred_element_type=jnp.float32)
        up_part = jnp.dot(normed, up_cols, preferred_element_type=jnp.float32)
        activated = (jax.nn.silu(gate_part) * up_part).astype(jnp.bfloat16)
        expert_out = jnp.dot(activated, w_down[expert * FF:(expert + 1) * FF], preferred_element_type=jnp.float32)
        weight_col = lax.optimization_barrier(jnp.sum(jnp.where(expert_ids == expert, gate_w, jnp.zeros_like(gate_w)), axis=1))
        moe_out = moe_out + weight_col[:, None] * expert_out
    mixed = (hidden_state + moe_out).astype(jnp.bfloat16)
    landed = jnp.zeros((REPLICAS,) + kv_cache.shape[1:], jnp.bfloat16)
    for migrant_pos in range(MIG):
        row_id = mig_rows[migrant_pos].astype(jnp.int32)
        kv_slab = seal(lax.dynamic_index_in_dim(kv_cache, row_id, 0, keepdims=False), lax.dynamic_index_in_dim(new_kv, row_id, 0, keepdims=False), lengths[row_id])
        landed = lax.dynamic_update_index_in_dim(landed, kv_slab, mig_dest[migrant_pos].astype(jnp.int32), 0)
    return (mixed, landed)
```

```python
import functools

import jax
import jax.numpy as jnp
from jax import lax
from jax.experimental import pallas as pl
from jax.experimental.pallas import tpu as pltpu
from jax.sharding import PartitionSpec as P

MESH = pl.DeviceIdType.MESH
F32 = jnp.float32
BF16 = jnp.bfloat16
D = 6144
BW = 768
ROWS = 8
HEADS = 6
HD = 128
SPAN = 384
HID = 256
PIECE = 48


def remote(src, dst, send_sem, recv_sem, grp, tp):
    return pltpu.make_async_remote_copy(
        src_ref=src,
        dst_ref=dst,
        send_sem=send_sem,
        recv_sem=recv_sem,
        device_id=(grp, tp),
        device_id_type=MESH,
    )


def kernel(
    lengths,
    eids,
    gates,
    mrows,
    mdest,
    q_hbm,
    kv_hbm,
    new_hbm,
    res_hbm,
    gain_ref,
    wo_hbm,
    wi_hbm,
    wd_hbm,
    mixed,
    landed,
    q_v,
    kv_v,
    new_v,
    res_v,
    wo_v,
    wi_v,
    wd_v,
    mig_out,
    mig_mid,
    mig_out2,
    gate_buf,
    rs_send,
    rs_recv,
    hid_v,
    sq_buf,
    y_buf,
    xb,
    act_v,
    acc_v,
    r1_send,
    r1_recv,
    r2_send,
    r2_recv,
    r3_send,
    r3_recv,
    r4_send,
    r4_recv,
    in_sem,
    wo_sem,
    loc_sem,
    mig_s,
    mig_r,
    mig2_s,
    mig2_r,
    gate_s,
    gate_r,
    rs_s,
    rs_r,
    sq_s,
    sq_r,
    ag1_s,
    ag1_r,
    ag2_s,
    ag2_r,
    ag3_s,
    ag3_r,
    ag4_s,
    ag4_r,
    r1_s,
    r1_r,
    r2_s,
    r2_r,
    r3_s,
    r3_r,
    r4_s,
    r4_r,
):
    g = lax.axis_index("grp")
    t = lax.axis_index("tp")
    z, x = g // 4, g % 4
    y, c = t // 2, t % 2
    second = jnp.where(c == 0, z, x)
    first = jnp.where(c == 0, x, z)
    me = second * 4 + first

    def grp_of(sec, fst):
        return jnp.where(c == 0, sec * 4 + fst, fst * 4 + sec)

    ins = [
        pltpu.make_async_copy(kv_hbm, kv_v, in_sem.at[0]),
        pltpu.make_async_copy(q_hbm, q_v, in_sem.at[1]),
        pltpu.make_async_copy(new_hbm, new_v, in_sem.at[2]),
        pltpu.make_async_copy(res_hbm, res_v, in_sem.at[3]),
    ]
    for cp in ins:
        cp.start()

    def wo_copy(i):
        b = (t + 1 + i) % 8
        return pltpu.make_async_copy(
            wo_hbm.at[:, pl.ds(pl.multiple_of(b * BW, BW), BW)], wo_v.at[i], wo_sem.at[i]
        )

    for i in range(8):
        wo_copy(i).start()
    wi_cp = pltpu.make_async_copy(wi_hbm.reshape(2 * D, HID), wi_v, in_sem.at[4])
    wi_cp.start()
    wd_cp = pltpu.make_async_copy(wd_hbm, wd_v, in_sem.at[5])
    wd_cp.start()

    barrier = pltpu.get_barrier_semaphore()

    @pl.loop(1, 8)
    def _(i):
        pl.semaphore_signal(barrier, inc=1, device_id=(g, (t + i) % 8), device_id_type=MESH)

    @pl.loop(1, 16)
    def _(i):
        pl.semaphore_signal(barrier, inc=1, device_id=((g + i) % 16, t), device_id_type=MESH)

    for cp in ins:
        cp.wait()
    qf = q_v[...].astype(F32).reshape(HEADS * ROWS, HD)
    qb = qf.astype(BF16)
    row_of = lax.broadcasted_iota(jnp.int32, (HEADS * ROWS, 1), 0) % ROWS
    scores = jnp.zeros((HEADS * ROWS, SPAN), F32)
    for r in range(ROWS):
        part = lax.dot_general(
            qb, kv_v[r, 0:SPAN, :], (((1,), (1,)), ((), ())), preferred_element_type=F32
        )
        scores = jnp.where(row_of == r, part, scores)
    scaling = HD ** (-0.5)
    scores = scores * scaling
    newf = new_v[...].astype(F32)
    new_k = jnp.concatenate([newf[:, 0, :]] * HEADS, axis=0)
    new_val = jnp.concatenate([newf[:, 1, :]] * HEADS, axis=0)
    own = jnp.sum(qf * new_k, axis=1, keepdims=True) * scaling
    span = jnp.zeros((HEADS * ROWS, 1), jnp.int32)
    for r in range(ROWS):
        span = jnp.where(row_of == r, lengths[r], span)
    seen = lax.broadcasted_iota(jnp.int32, (HEADS * ROWS, SPAN), 1) < span
    top = jnp.maximum(
        jnp.max(jnp.where(seen, scores, -jnp.inf), axis=1, keepdims=True), own
    )
    spread = jnp.where(seen, jnp.exp(scores - top), 0.0)
    own_exp = jnp.exp(own - top)
    denom = jnp.sum(spread, axis=1, keepdims=True) + own_exp
    weights = (spread / denom).astype(BF16)
    own_w = (own_exp / denom).astype(BF16).astype(F32)
    mix = jnp.zeros((HEADS * ROWS, HD), F32)
    for r in range(ROWS):
        part = jnp.dot(weights, kv_v[r, SPAN : 2 * SPAN, :], preferred_element_type=F32)
        mix = jnp.where(row_of == r, part, mix)
    mix = mix + own_w * new_val
    heads = jnp.concatenate(
        [mix[h * ROWS : (h + 1) * ROWS] for h in range(HEADS)], axis=1
    ).astype(BF16)

    sub = lax.broadcasted_iota(jnp.int32, (ROWS, 128), 0)
    lane = lax.broadcasted_iota(jnp.int32, (ROWS, 128), 1)
    gate_rows = jnp.zeros((ROWS, 128), F32)
    for r in range(ROWS):
        for k in range(2):
            gate_rows = jnp.where(
                jnp.logical_and(sub == r, lane == eids[k, r]), gates[k, r], gate_rows
            )
    gate_buf[g] = gate_rows

    row = jnp.int32(0)
    leaves = jnp.int32(0)
    for i in range(8):
        hit = (mrows[i] >> 3) == g
        row = row + jnp.where(hit, mrows[i] & 7, 0)
        leaves = leaves + jnp.where(hit, 1, 0)
    limit = jnp.int32(0)
    fresh_k = jnp.zeros((1, HD), F32)
    fresh_v = jnp.zeros((1, HD), F32)
    for r in range(ROWS):
        limit = limit + jnp.where(row == r, lengths[r], 0)
        fresh_k = jnp.where(row == r, new_k[r : r + 1], fresh_k)
        fresh_v = jnp.where(row == r, new_val[r : r + 1], fresh_v)
    limit = jnp.where(leaves > 0, limit, -1)

    def sealed(k):
        pos = lax.broadcasted_iota(jnp.int32, (PIECE, HD), 0) + (k % 8) * PIECE
        old = kv_v[row, pl.ds(pl.multiple_of(k * PIECE, PIECE), PIECE), :].astype(F32)
        fresh = jnp.where(k < 8, fresh_k, fresh_v)
        return jnp.where(
            pos < limit, old, jnp.where(pos == limit, fresh, 0.0)
        ).astype(BF16)

    def seal_step(k, _):
        mig_out[k] = sealed(k)
        return 0

    lax.fori_loop(0, 16, seal_step, 0)
    mig_mid[g] = mig_out[g]

    pl.semaphore_wait(barrier, 22)

    def rs_copy(i):
        b = (t + 1 + i) % 8
        return remote(rs_send.at[i], rs_recv.at[t], rs_s.at[i], rs_r.at[t], g, b)

    def proj_step(i, _):
        wo_copy(i).wait()
        part = jnp.dot(heads, wo_v[i], preferred_element_type=F32)
        rs_send[i] = part.astype(BF16)
        rs_copy(i).start()
        return 0

    lax.fori_loop(0, 7, proj_step, 0)
    wo_copy(7).wait()
    attended = jnp.dot(heads, wo_v[7], preferred_element_type=F32)

    def gate_copy(i):
        return remote(
            gate_buf.at[g], gate_buf.at[g], gate_s.at[i], gate_r.at[g], (g + i) % 16, t
        )

    def mig_copy(i):
        k = (g + i) % 16
        return remote(mig_out.at[k], mig_mid.at[g], mig_s.at[i], mig_r.at[g], k, t)

    @pl.loop(1, 16)
    def _(i):
        gate_copy(i).start()
        mig_copy(i).start()

    hidden = res_v[...].astype(F32) + attended
    for i in range(1, 8):
        p = (t + i) % 8
        remote(rs_recv.at[p], rs_recv.at[p], rs_s.at[0], rs_r.at[p], g, t).wait_recv()
        hidden = hidden + rs_recv[p].astype(F32)
    hid_v[...] = hidden
    squares = jnp.sum(hidden * hidden, axis=1, keepdims=True)
    sq_buf[t] = jnp.broadcast_to(squares, (ROWS, 128))

    def sq_copy(i):
        return remote(
            sq_buf.at[t], sq_buf.at[t], sq_s.at[i], sq_r.at[t], g, (t + i) % 8
        )

    for i in range(1, 8):
        sq_copy(i).start()
    gain = gain_ref[...].astype(F32)
    scaled = hidden * gain
    ri = lax.broadcasted_iota(jnp.int32, (128, 128), 0)
    ci = lax.broadcasted_iota(jnp.int32, (128, 128), 1)
    spot = jnp.where(ri < 64, 2 * ri, 2 * ri - 127)
    shuffle = jnp.where(spot == ci, 1.0, 0.0).astype(BF16)
    stacked = jnp.concatenate(
        [scaled[:, k * 128 : (k + 1) * 128] for k in range(6)], axis=0
    ).astype(BF16)
    stacked = jnp.dot(stacked, shuffle, preferred_element_type=F32)
    y_buf[y] = jnp.concatenate(
        [stacked[k * ROWS : (k + 1) * ROWS] for k in range(6)], axis=1
    ).astype(BF16)

    def ag1_copy(i):
        q = (y + i) % 4
        return remote(
            y_buf.at[y], y_buf.at[y], ag1_s.at[i], ag1_r.at[y], g, q * 2 + c
        )

    for i in range(1, 4):
        ag1_copy(i).start()

    total = squares
    for i in range(1, 8):
        p = (t + i) % 8
        remote(sq_buf.at[p], sq_buf.at[p], sq_s.at[0], sq_r.at[p], g, t).wait_recv()
        total = total + sq_buf[p][:, 0:1]
    scale = lax.rsqrt(total / D + 1e-05)
    for i in range(4):
        p = (y + i) % 4
        if i > 0:
            remote(
                y_buf.at[p], y_buf.at[p], ag1_s.at[0], ag1_r.at[p], g, t
            ).wait_recv()
        xb[c, p, me] = (y_buf[p].astype(F32) * scale).astype(BF16)

    def ag2_copy(i):
        f = (first + i) % 4
        return remote(
            xb.at[c, :, me],
            xb.at[c, :, me],
            ag2_s.at[i],
            ag2_r.at[first],
            grp_of(second, f),
            t,
        )

    for i in range(1, 4):
        ag2_copy(i).start()

    def mig_recv(i):
        s = (g + i) % 16
        return remote(mig_mid.at[s], mig_mid.at[s], mig_s.at[0], mig_r.at[s], g, t)

    @pl.loop(1, 16)
    def _(i):
        mig_recv(i).wait_recv()

    def mig2_copy(j):
        return remote(mig_out2.at[j], landed.at[g], mig2_s.at[j], mig2_r.at[g], j, t)

    def route_step(i, _):
        j = (g + i) % 16
        src = jnp.int32(0)
        some = jnp.int32(0)
        for k in range(8):
            hit = mdest[k] == j
            src = src + jnp.where(hit, mrows[k] >> 3, 0)
            some = some + jnp.where(hit, 1, 0)
        piece = mig_mid[src].astype(F32)
        mig_out2[j] = jnp.where(some > 0, piece, 0.0).astype(BF16)

        @pl.when(i > 0)
        def _():
            mig2_copy(j).start()

        return 0

    lax.fori_loop(0, 16, route_step, 0)
    keep = pltpu.make_async_copy(mig_out2.at[g], landed.at[g], loc_sem)
    keep.start()

    for i in range(1, 4):
        f = (first + i) % 4
        slot = second * 4 + f
        remote(
            xb.at[c, :, slot], xb.at[c, :, slot], ag2_s.at[0], ag2_r.at[f], g, t
        ).wait_recv()

    def ag3_copy(i, yb):
        mine = pl.ds(second * 4, 4)
        s = (second + i) % 4
        return remote(
            xb.at[c, yb, mine],
            xb.at[c, yb, mine],
            ag3_s.at[yb, i],
            ag3_r.at[yb, second],
            grp_of(s, first),
            t,
        )

    for yb in range(4):
        for i in range(1, 4):
            ag3_copy(i, yb).start()

    partner = y * 2 + 1 - c

    def ag4_copy(yb):
        return remote(
            xb.at[c, yb], xb.at[c, yb], ag4_s.at[yb], ag4_r.at[yb], g, partner
        )

    wi_cp.wait()
    even = lax.broadcasted_iota(jnp.int32, (128, 128), 1) % 2 == 0

    def slot_of(h, zz, xx):
        return jnp.where(h == 0, zz * 4 + xx, xx * 4 + zz)

    def up_part(h, yb):
        blocks = [
            xb[h, yb, slot_of(h, k // 4, k % 4)].astype(F32) for k in range(16)
        ]
        rows = jnp.concatenate(blocks, axis=0)
        gate_lhs, up_lhs = [], []
        for k in range(6):
            v = rows[:, k * 128 : (k + 1) * 128]
            back = pltpu.roll(v, 127, 1)
            ahead = pltpu.roll(v, 1, 1)
            gate_lhs += [jnp.where(even, v, 0.0), jnp.where(even, back, 0.0)]
            up_lhs += [jnp.where(even, 0.0, ahead), jnp.where(even, 0.0, v)]
        lhs = jnp.concatenate(
            [
                jnp.concatenate(gate_lhs, axis=1).astype(BF16),
                jnp.concatenate(up_lhs, axis=1).astype(BF16),
            ],
            axis=0,
        )
        b = yb * 2 + h
        rhs = wi_v[pl.ds(pl.multiple_of(b * 2 * BW, 2 * BW), 2 * BW), :]
        acc_v[...] += jnp.dot(lhs, rhs, preferred_element_type=F32)

    acc_v[...] = jnp.zeros_like(acc_v)

    def up_step(yb, _):
        @pl.when(yb < 4)
        def _():
            for i in range(1, 4):
                s = (second + i) % 4
                theirs = pl.ds(s * 4, 4)
                remote(
                    xb.at[c, yb, theirs],
                    xb.at[c, yb, theirs],
                    ag3_s.at[yb, 0],
                    ag3_r.at[yb, s],
                    g,
                    t,
                ).wait_recv()
            ag4_copy(yb).start()
            up_part(c, yb)

        @pl.when(yb > 0)
        def _():
            old = yb - 1
            remote(
                xb.at[1 - c, old],
                xb.at[1 - c, old],
                ag4_s.at[old],
                ag4_r.at[old],
                g,
                t,
            ).wait_recv()
            up_part(1 - c, old)

        return 0

    lax.fori_loop(0, 5, up_step, 0)

    @pl.loop(1, 16)
    def _(i):
        s = (g + i) % 16
        remote(
            gate_buf.at[s], gate_buf.at[s], gate_s.at[0], gate_r.at[s], g, t
        ).wait_recv()

    gate_all = jnp.concatenate([gate_buf[k] for k in range(16)], axis=0)
    expert = g // 4
    lane_all = lax.broadcasted_iota(jnp.int32, (128, 128), 1)
    gate_col = jnp.sum(
        jnp.where(lane_all == expert, gate_all, 0.0), axis=1, keepdims=True
    )
    gate_part = acc_v[0:128, :]
    up_value = acc_v[128:256, :]
    silu = gate_part / (1.0 + jnp.exp(-gate_part))
    act_v[...] = (silu * up_value * gate_col).astype(BF16)

    wd_cp.wait()

    def down(h, yb):
        b = yb * 2 + h
        cols = pl.ds(pl.multiple_of(b * BW, BW), BW)
        return jnp.dot(act_v[...], wd_v[:, cols], preferred_element_type=F32)

    def r1_copy(yb):
        return remote(
            r1_send.at[yb], r1_recv.at[yb], r1_s.at[yb], r1_r.at[yb], g, partner
        )

    def r1_step(yb, _):
        h = 1 - c
        part = down(h, yb)
        for k in range(16):
            r1_send[yb, slot_of(h, k // 4, k % 4)] = part[
                k * ROWS : (k + 1) * ROWS
            ].astype(BF16)
        r1_copy(yb).start()
        return 0

    lax.fori_loop(0, 4, r1_step, 0)

    def r2_copy(i, yb):
        s = (second + i) % 4
        return remote(
            r2_send.at[yb, pl.ds(s * 4, 4)],
            r2_recv.at[second, yb],
            r2_s.at[yb, i],
            r2_r.at[yb, second],
            grp_of(s, first),
            t,
        )

    def r2_step(yb, _):
        part = down(c, yb)
        remote(
            r1_recv.at[yb], r1_recv.at[yb], r1_s.at[yb], r1_r.at[yb], g, t
        ).wait_recv()
        for k in range(16):
            slot = slot_of(c, k // 4, k % 4)
            both = part[k * ROWS : (k + 1) * ROWS] + r1_recv[yb, slot].astype(F32)
            r2_send[yb, slot] = both.astype(BF16)
        for i in range(1, 4):
            r2_copy(i, yb).start()
        return 0

    lax.fori_loop(0, 4, r2_step, 0)

    def r2_sum(yb, _):
        total2 = r2_send[yb, pl.ds(second * 4, 4)].astype(F32)
        for i in range(1, 4):
            s = (second + i) % 4
            remote(
                r2_recv.at[s, yb],
                r2_recv.at[s, yb],
                r2_s.at[yb, 0],
                r2_r.at[yb, s],
                g,
                t,
            ).wait_recv()
            total2 = total2 + r2_recv[s, yb].astype(F32)
        r3_send[:, yb] = total2.astype(BF16)
        return 0

    lax.fori_loop(0, 4, r2_sum, 0)

    def r3_copy(i):
        f = (first + i) % 4
        return remote(
            r3_send.at[f],
            r3_recv.at[first],
            r3_s.at[i],
            r3_r.at[first],
            grp_of(second, f),
            t,
        )

    for i in range(1, 4):
        r3_copy(i).start()
    total3 = r3_send[first].astype(F32)
    for i in range(1, 4):
        f = (first + i) % 4
        remote(
            r3_recv.at[f], r3_recv.at[f], r3_s.at[0], r3_r.at[f], g, t
        ).wait_recv()
        total3 = total3 + r3_recv[f].astype(F32)
    r4_send[...] = total3.astype(BF16)

    def r4_copy(i):
        q = (y + i) % 4
        return remote(
            r4_send.at[q], r4_recv.at[y], r4_s.at[i], r4_r.at[y], g, q * 2 + c
        )

    for i in range(1, 4):
        r4_copy(i).start()
    result = hid_v[...] + r4_send[y].astype(F32)
    for i in range(1, 4):
        q = (y + i) % 4
        remote(
            r4_recv.at[q], r4_recv.at[q], r4_s.at[0], r4_r.at[q], g, t
        ).wait_recv()
        result = result + r4_recv[q].astype(F32)
    mixed[...] = result.astype(BF16)

    keep.wait()

    @pl.loop(1, 16)
    def _(i):
        s = (g + i) % 16
        remote(
            landed.at[s], landed.at[s], mig2_s.at[0], mig2_r.at[s], g, t
        ).wait_recv()
        mig2_copy(s).wait_send()
        mig_copy(i).wait_send()
        gate_copy(i).wait_send()

    for i in range(7):
        rs_copy(i).wait_send()
        sq_copy(i + 1).wait_send()
    for i in range(1, 4):
        ag1_copy(i).wait_send()
        ag2_copy(i).wait_send()
        r3_copy(i).wait_send()
        r4_copy(i).wait_send()

    @pl.loop(0, 4)
    def _(yb):
        ag4_copy(yb).wait_send()
        r1_copy(yb).wait_send()
        for i in range(1, 4):
            ag3_copy(i, yb).wait_send()
            r2_copy(i, yb).wait_send()


def body(
    queries,
    kv_cache,
    new_kv,
    lengths,
    residual,
    w_out,
    norm_gain,
    expert_ids,
    gate_w,
    w_inner,
    w_down,
    mig_rows,
    mig_dest,
):
    vmem = pltpu.VMEM
    dma = pltpu.SemaphoreType.DMA
    smem_spec = pl.BlockSpec(memory_space=pltpu.SMEM)
    any_spec = pl.BlockSpec(memory_space=pl.ANY)
    vmem_spec = pl.BlockSpec(memory_space=pltpu.VMEM)
    mixed, landed = pl.pallas_call(
        kernel,
        out_shape=(
            jax.ShapeDtypeStruct((ROWS, BW), BF16),
            jax.ShapeDtypeStruct((16, PIECE, HD), BF16),
        ),
        in_specs=[smem_spec] * 5 + [any_spec] * 4 + [vmem_spec] + [any_spec] * 3,
        out_specs=(vmem_spec, any_spec),
        scratch_shapes=[
            vmem((HEADS, ROWS, HD), BF16),
            vmem((ROWS, 2 * SPAN, HD), BF16),
            vmem((ROWS, 2, HD), BF16),
            vmem((ROWS, BW), BF16),
            vmem((8, BW, BW), BF16),
            vmem((2 * D, HID), BF16),
            vmem((HID, D), BF16),
            vmem((16, PIECE, HD), BF16),
            vmem((16, PIECE, HD), BF16),
            vmem((16, PIECE, HD), BF16),
            vmem((16, ROWS, 128), F32),
            vmem((8, ROWS, BW), BF16),
            vmem((8, ROWS, BW), BF16),
            vmem((ROWS, BW), F32),
            vmem((8, ROWS, 128), F32),
            vmem((4, ROWS, BW), BF16),
            vmem((2, 4, 16, ROWS, BW), BF16),
            vmem((128, HID), BF16),
            vmem((256, HID), F32),
            vmem((4, 16, ROWS, BW), BF16),
            vmem((4, 16, ROWS, BW), BF16),
            vmem((4, 16, ROWS, BW), BF16),
            vmem((4, 4, 4, ROWS, BW), BF16),
            vmem((4, 4, ROWS, BW), BF16),
            vmem((4, 4, ROWS, BW), BF16),
            vmem((4, ROWS, BW), BF16),
            vmem((4, ROWS, BW), BF16),
            dma((6,)),
            dma((8,)),
            dma,
            dma((16,)),
            dma((16,)),
            dma((16,)),
            dma((16,)),
            dma((16,)),
            dma((16,)),
            dma((8,)),
            dma((8,)),
            dma((8,)),
            dma((8,)),
            dma((4,)),
            dma((4,)),
            dma((4,)),
            dma((4,)),
            dma((4, 4)),
            dma((4, 4)),
            dma((4,)),
            dma((4,)),
            dma((4,)),
            dma((4,)),
            dma((4, 4)),
            dma((4, 4)),
            dma((4,)),
            dma((4,)),
            dma((4,)),
            dma((4,)),
        ],
        compiler_params=pltpu.CompilerParams(
            collective_id=0,
            has_side_effects=True,
            vmem_limit_bytes=56 * 2**20,
        ),
        cost_estimate=pl.CostEstimate(
            flops=2 * (8 * BW * D + 256 * 2 * D * HID + 128 * HID * D),
            bytes_accessed=21 * 10**6,
            transcendentals=128 * HID,
        ),
    )(
        lengths,
        expert_ids.T,
        gate_w.T,
        mig_rows,
        mig_dest,
        queries.transpose(1, 0, 2),
        kv_cache.reshape(ROWS, 2 * SPAN, HD),
        new_kv.reshape(ROWS, 2, HD),
        residual,
        norm_gain.astype(F32).reshape(1, BW),
        w_out,
        w_inner,
        w_down,
    )
    return mixed, landed.reshape(1, 2, 1, SPAN, HD)


def solution(mesh):
    in_specs = (
        P("grp", "tp", None),
        P("grp", None, "tp", None, None),
        P("grp", None, "tp", None),
        P("grp"),
        P("grp", "tp"),
        P("tp", None),
        P("tp"),
        P("grp", None),
        P("grp", None),
        P(None, None, ("grp", "tp")),
        P(("grp", "tp"), None),
        P(),
        P(),
    )
    out_specs = (P("grp", "tp"), P("grp", None, "tp", None, None))
    return jax.shard_map(body, mesh=mesh, in_specs=in_specs, out_specs=out_specs, check_vma=False)
```

```python
import functools

import jax
import jax.numpy as jnp
from jax import lax
from jax.experimental import pallas as pl
from jax.experimental.pallas import tpu as pltpu
from jax.sharding import PartitionSpec as P

MESH = pl.DeviceIdType.MESH
F32 = jnp.float32
BF16 = jnp.bfloat16
D = 6144
EXPERTS = 4
BW = 768
ROWS = 8
HEADS = 6
HD = 128
SPAN = 384
HID = 256
PIECE = 48


def remote(src, dst, send_sem, recv_sem, grp, tp):
    return pltpu.make_async_remote_copy(
        src_ref=src,
        dst_ref=dst,
        send_sem=send_sem,
        recv_sem=recv_sem,
        device_id=(grp, tp),
        device_id_type=MESH,
    )


def kernel(
    len_hbm,
    eids_hbm,
    gates_hbm,
    mrows_hbm,
    mdest_hbm,
    q_hbm,
    kv_hbm,
    new_hbm,
    res_hbm,
    gain_hbm,
    wo_hbm,
    wi_hbm,
    wd_hbm,
    mixed,
    landed,
    lengths,
    eids,
    gates,
    mrows,
    mdest,
    q_v,
    kv_v,
    new_v,
    res_v,
    gain_ref,
    wo_v,
    wi_v,
    wd_v,
    mig_out,
    mig_mid,
    mig_out2,
    gate_buf,
    gain_buf,
    p_send,
    p_recv,
    sum_v,
    a_send,
    a_recv,
    hid_v,
    sq_buf,
    xb,
    act_v,
    acc_v,
    r1_send,
    r1_recv,
    r2_send,
    r2_recv,
    in_sem,
    wo_sem,
    loc_sem,
    mig_s,
    mig_r,
    mig2_s,
    mig2_r,
    gate_s,
    gate_r,
    gain_s,
    gain_r,
    p_s,
    p_r,
    a_s,
    a_r,
    sq_s,
    sq_r,
    ag_s,
    ag_r,
    agc_s,
    agc_r,
    r1_s,
    r1_r,
    r2_s,
    r2_r,
    ready,
):
    g = lax.axis_index("grp")
    t = lax.axis_index("tp")
    z, x = g // 4, g % 4
    y, c = t // 2, t % 2
    partner = y * 2 + 1 - c

    def taken(ref, sem):
        remote(ref, ref, sem, sem, g, t).wait_recv()

    def sent(ref, sem):
        remote(ref, ref, sem, sem, g, t).wait_send()

    ins = [
        pltpu.make_async_copy(kv_hbm, kv_v, in_sem.at[0]),
        pltpu.make_async_copy(q_hbm, q_v, in_sem.at[1]),
        pltpu.make_async_copy(new_hbm, new_v, in_sem.at[2]),
        pltpu.make_async_copy(res_hbm, res_v, in_sem.at[3]),
        pltpu.make_async_copy(len_hbm, lengths, in_sem.at[6]),
        pltpu.make_async_copy(eids_hbm, eids, in_sem.at[7]),
        pltpu.make_async_copy(gates_hbm, gates, in_sem.at[8]),
        pltpu.make_async_copy(mrows_hbm, mrows, in_sem.at[9]),
        pltpu.make_async_copy(mdest_hbm, mdest, in_sem.at[10]),
        pltpu.make_async_copy(gain_hbm, gain_ref, in_sem.at[11]),
    ]
    for cp in ins:
        cp.start()

    def wo_copy(i):
        b = (i % 4) * 2 + (1 - c if i < 4 else c)
        return pltpu.make_async_copy(
            wo_hbm.at[:, pl.ds(pl.multiple_of(b * BW, BW), BW)], wo_v.at[i], wo_sem.at[i]
        )

    wi_cp = pltpu.make_async_copy(wi_hbm.reshape(2 * D, HID), wi_v, in_sem.at[4])
    wd_cp = pltpu.make_async_copy(wd_hbm, wd_v, in_sem.at[5])
    for i in range(3):
        wo_copy(i).start()

    barrier = pltpu.get_barrier_semaphore()

    def greet(sem, grp, tp):
        pl.semaphore_signal(sem, inc=1, device_id=(grp, tp), device_id_type=MESH)

    greet(barrier, g, partner)
    for d in range(1, 4):
        greet(barrier, g, ((y + d) % 4) * 2 + c)
        greet(barrier, (g + 4 * d) % 16, t)
        greet(barrier, z * 4 + (x + d) % 4, t)

    for cp in ins:
        cp.wait()
    wo_copy(3).start()
    qf = q_v[...].astype(F32).reshape(HEADS * ROWS, HD)
    qb = qf.astype(BF16)
    row_of = lax.broadcasted_iota(jnp.int32, (HEADS * ROWS, 1), 0) % ROWS
    scores = jnp.zeros((HEADS * ROWS, SPAN), F32)
    for r in range(ROWS):
        part = lax.dot_general(
            qb, kv_v[r, 0:SPAN, :], (((1,), (1,)), ((), ())), preferred_element_type=F32
        )
        scores = jnp.where(row_of == r, part, scores)
    wo_copy(4).start()
    scaling = HD ** (-0.5)
    scores = scores * scaling
    newf = new_v[...].astype(F32)
    new_k = jnp.concatenate([newf[:, 0, :]] * HEADS, axis=0)
    new_val = jnp.concatenate([newf[:, 1, :]] * HEADS, axis=0)
    own = jnp.sum(qf * new_k, axis=1, keepdims=True) * scaling
    span = jnp.zeros((HEADS * ROWS, 1), jnp.int32)
    for r in range(ROWS):
        span = jnp.where(row_of == r, lengths[r], span)
    seen = lax.broadcasted_iota(jnp.int32, (HEADS * ROWS, SPAN), 1) < span
    top = jnp.maximum(
        jnp.max(jnp.where(seen, scores, -jnp.inf), axis=1, keepdims=True), own
    )
    spread = jnp.where(seen, jnp.exp(scores - top), 0.0)
    own_exp = jnp.exp(own - top)
    denom = jnp.sum(spread, axis=1, keepdims=True) + own_exp
    weights = (spread / denom).astype(BF16)
    own_w = (own_exp / denom).astype(BF16).astype(F32)
    wo_copy(5).start()
    mix = jnp.zeros((HEADS * ROWS, HD), F32)
    for r in range(ROWS):
        part = jnp.dot(weights, kv_v[r, SPAN : 2 * SPAN, :], preferred_element_type=F32)
        mix = jnp.where(row_of == r, part, mix)
    mix = mix + own_w * new_val
    heads = jnp.concatenate(
        [mix[h * ROWS : (h + 1) * ROWS] for h in range(HEADS)], axis=1
    ).astype(BF16)
    wo_copy(6).start()
    wo_copy(7).start()

    row = jnp.int32(0)
    leaves = jnp.int32(0)
    for i in range(8):
        hit = (mrows[i] >> 3) == g
        row = row + jnp.where(hit, mrows[i] & 7, 0)
        leaves = leaves + jnp.where(hit, 1, 0)
    limit = jnp.int32(0)
    fresh_k = jnp.zeros((1, HD), F32)
    fresh_v = jnp.zeros((1, HD), F32)
    for r in range(ROWS):
        limit = limit + jnp.where(row == r, lengths[r], 0)
        fresh_k = jnp.where(row == r, new_k[r : r + 1], fresh_k)
        fresh_v = jnp.where(row == r, new_val[r : r + 1], fresh_v)
    limit = jnp.where(leaves > 0, limit, -1)

    def sealed(k):
        pos = lax.broadcasted_iota(jnp.int32, (PIECE, HD), 0) + (k % 8) * PIECE
        old = kv_v[row, pl.ds(pl.multiple_of(k * PIECE, PIECE), PIECE), :].astype(F32)
        fresh = jnp.where(k < 8, fresh_k, fresh_v)
        return jnp.where(
            pos < limit, old, jnp.where(pos == limit, fresh, 0.0)
        ).astype(BF16)

    def seal_step(k, _):
        mig_out[k] = sealed(k)
        return 0

    lax.fori_loop(0, 16, seal_step, 0)
    mig_mid[g] = mig_out[g]
    gain_buf[y] = jnp.broadcast_to(
        gain_ref[...].astype(F32).reshape(1, BW), (ROWS, BW)
    ).astype(BF16)

    for i in range(4):
        wo_copy(i).wait()
        p_send[i] = jnp.dot(heads, wo_v[i], preferred_element_type=F32).astype(BF16)

    pl.semaphore_wait(barrier, 10)
    for d in range(1, 4):
        greet(ready, z * 4 + (x + d) % 4, t)

    def p_copy(i):
        return remote(p_send.at[i], p_recv.at[i], p_s, p_r.at[i], g, partner)

    def a_copy(i, d):
        q = (y + d) % 4
        return remote(a_send.at[i], a_recv.at[i, y], a_s, a_r.at[i], g, q * 2 + c)

    def gain_copy(d):
        q = (y + d) % 4
        return remote(gain_buf.at[y], gain_buf.at[y], gain_s, gain_r, g, q * 2 + c)

    def mig_copy(i):
        k = (g + i) % 16
        return remote(mig_out.at[k], mig_mid.at[g], mig_s, mig_r, k, t)

    for i in range(4):
        p_copy(i).start()
    for d in range(1, 4):
        gain_copy(d).start()
    wi_cp.start()
    wd_cp.start()
    for i in range(4):
        wo_copy(i + 4).wait()
        part = jnp.dot(heads, wo_v[i + 4], preferred_element_type=F32)
        taken(p_recv.at[i], p_r.at[i])
        part = part + p_recv[i].astype(F32)
        part = part + jnp.where(y == i, res_v[...].astype(F32), 0.0)
        sum_v[i] = part
        a_send[i] = part.astype(BF16)
        for d in range(1, 4):
            a_copy(i, d).start()

    pl.semaphore_wait(ready, 3)

    @pl.loop(1, 16)
    def _(i):
        mig_copy(i).start()

    sub = lax.broadcasted_iota(jnp.int32, (ROWS, 128), 0)
    lane = lax.broadcasted_iota(jnp.int32, (ROWS, 128), 1)
    gate_rows = jnp.zeros((ROWS, 128), F32)
    for r in range(ROWS):
        for k in range(2):
            gate_rows = jnp.where(
                jnp.logical_and(sub == r, lane == eids[k, r]), gates[k, r], gate_rows
            )

    ri = lax.broadcasted_iota(jnp.int32, (128, 128), 0)
    ci = lax.broadcasted_iota(jnp.int32, (128, 128), 1)
    spot = jnp.where(ri < 64, 2 * ri, 2 * ri - 127)
    shuffle = jnp.where(spot == ci, 1.0, 0.0).astype(BF16)

    def ag_copy(i, d):
        return remote(
            xb.at[c, i, g], xb.at[c, i, g], ag_s, ag_r.at[i], (g + d) % 16, t
        )

    taken(gain_buf.at[pl.ds(0, 3)], gain_r)
    squares = jnp.zeros((ROWS, 1), F32)
    for i in range(4):
        taken(a_recv.at[i, pl.ds(0, 3)], a_r.at[i])
        hidden = sum_v[i]
        for d in range(1, 4):
            hidden = hidden + a_recv[i, (y + d) % 4].astype(F32)
        hid_v[i] = hidden
        squares = squares + jnp.sum(hidden * hidden, axis=1, keepdims=True)
        scaled = hidden * gain_buf[i].astype(F32)
        stacked = jnp.concatenate(
            [scaled[:, k * 128 : (k + 1) * 128] for k in range(6)], axis=0
        ).astype(BF16)
        stacked = jnp.dot(stacked, shuffle, preferred_element_type=F32)
        xb[c, i, g] = jnp.concatenate(
            [stacked[k * ROWS : (k + 1) * ROWS] for k in range(6)], axis=1
        ).astype(BF16)

        @pl.loop(1, 16)
        def _(d):
            ag_copy(i, d).start()

    sq_buf[0] = jnp.broadcast_to(squares, (ROWS, 128))
    sq_copy = remote(sq_buf.at[0], sq_buf.at[1], sq_s, sq_r, g, partner)
    sq_copy.start()
    taken(sq_buf.at[1], sq_r)
    scale = lax.rsqrt((sq_buf[0] + sq_buf[1]) / D + 1e-05)
    gate_buf[g] = jnp.where(lane == EXPERTS, scale, gate_rows)

    def gate_copy(i):
        return remote(
            gate_buf.at[g], gate_buf.at[g], gate_s, gate_r, (g + i) % 16, t
        )

    @pl.loop(1, 16)
    def _(i):
        gate_copy(i).start()

    taken(mig_mid.at[pl.ds(0, 15)], mig_r)

    def mig2_copy(j):
        return remote(mig_out2.at[j], landed.at[g], mig2_s, mig2_r, j, t)

    def route_step(i, _):
        j = (g + i) % 16
        src = jnp.int32(0)
        some = jnp.int32(0)
        for k in range(8):
            hit = mdest[k] == j
            src = src + jnp.where(hit, mrows[k] >> 3, 0)
            some = some + jnp.where(hit, 1, 0)
        piece = mig_mid[src].astype(F32)
        mig_out2[j] = jnp.where(some > 0, piece, 0.0).astype(BF16)

        @pl.when(i > 0)
        def _():
            mig2_copy(j).start()

        return 0

    lax.fori_loop(0, 16, route_step, 0)
    keep = pltpu.make_async_copy(mig_out2.at[g], landed.at[g], loc_sem)
    keep.start()

    sent(p_send, p_s)
    sent(a_recv.at[pl.ds(0, 3)], a_s)
    sent(gain_buf.at[pl.ds(0, 3)], gain_s)
    sent(mig_out.at[pl.ds(0, 15)], mig_s)
    sent(sq_buf.at[0], sq_s)

    wi_cp.wait()
    even = lax.broadcasted_iota(jnp.int32, (128, 128), 1) % 2 == 0

    def agc_copy(i):
        return remote(xb.at[c, i], xb.at[c, i], agc_s, agc_r.at[i], g, partner)

    def up_part(h, yb):
        rows = jnp.concatenate(
            [xb[h, yb, k].astype(F32) for k in range(16)], axis=0
        )
        gate_lhs, up_lhs = [], []
        for k in range(6):
            v = rows[:, k * 128 : (k + 1) * 128]
            back = pltpu.roll(v, 127, 1)
            ahead = pltpu.roll(v, 1, 1)
            gate_lhs += [jnp.where(even, v, 0.0), jnp.where(even, back, 0.0)]
            up_lhs += [jnp.where(even, 0.0, ahead), jnp.where(even, 0.0, v)]
        lhs = jnp.concatenate(
            [
                jnp.concatenate(gate_lhs, axis=1).astype(BF16),
                jnp.concatenate(up_lhs, axis=1).astype(BF16),
            ],
            axis=0,
        )
        b = yb * 2 + h
        rhs = wi_v[pl.ds(pl.multiple_of(b * 2 * BW, 2 * BW), 2 * BW), :]
        acc_v[...] += jnp.dot(lhs, rhs, preferred_element_type=F32)

    acc_v[...] = jnp.zeros_like(acc_v)

    def up_step(yb, _):
        @pl.when(yb < 4)
        def _():
            taken(xb.at[c, yb, pl.ds(0, 15)], ag_r.at[yb])
            agc_copy(yb).start()
            up_part(c, yb)

        @pl.when(yb > 0)
        def _():
            taken(xb.at[1 - c, yb - 1], agc_r.at[yb - 1])
            up_part(1 - c, yb - 1)

        return 0

    lax.fori_loop(0, 5, up_step, 0)

    taken(gate_buf.at[pl.ds(0, 15)], gate_r)
    gate_all = jnp.concatenate([gate_buf[k] for k in range(16)], axis=0)
    expert = g // 4
    lane_all = lax.broadcasted_iota(jnp.int32, (128, 128), 1)
    gate_col = jnp.sum(
        jnp.where(lane_all == expert, gate_all, 0.0), axis=1, keepdims=True
    )
    scale_col = gate_all[:, EXPERTS : EXPERTS + 1]
    gate_part = acc_v[0:128, :] * scale_col
    up_value = acc_v[128:256, :] * scale_col
    silu = gate_part / (1.0 + jnp.exp(-gate_part))
    act_v[...] = (silu * up_value * gate_col).astype(BF16)

    wd_cp.wait()

    def down(h, yb):
        b = yb * 2 + h
        cols = pl.ds(pl.multiple_of(b * BW, BW), BW)
        return jnp.dot(act_v[...], wd_v[:, cols], preferred_element_type=F32)

    def r1_copy(yb):
        return remote(r1_send.at[yb], r1_recv.at[yb], r1_s, r1_r.at[yb], g, partner)

    def r1_step(j, _):
        yb = (y + 1 + j) % 4
        part = down(1 - c, yb)
        for k in range(16):
            r1_send[yb, k] = part[k * ROWS : (k + 1) * ROWS].astype(BF16)
        r1_copy(yb).start()
        return 0

    lax.fori_loop(0, 4, r1_step, 0)

    def r2_copy(j, yb, k):
        return remote(
            r2_send.at[yb, k], r2_recv.at[y, g], r2_s.at[j // 3], r2_r.at[y], k, yb * 2 + c
        )

    def r2_step(j, _):
        yb = (y + 1 + j) % 4
        part = down(c, yb)
        taken(r1_recv.at[yb], r1_r.at[yb])
        for k in range(16):
            both = part[k * ROWS : (k + 1) * ROWS] + r1_recv[yb, k].astype(F32)
            r2_send[yb, k] = both.astype(BF16)

        @pl.loop(1, 16)
        def _(i):
            r2_copy(j, yb, (g + i) % 16).start()

        @pl.when(j < 3)
        def _():
            r2_copy(j, yb, g).start()

        return 0

    lax.fori_loop(0, 4, r2_step, 0)

    keep.wait()
    taken(landed.at[pl.ds(0, 15)], mig2_r)
    sent(mig_out2.at[pl.ds(0, 15)], mig2_s)
    sent(gate_buf.at[pl.ds(0, 15)], gate_s)
    sent(xb.at[0, :, pl.ds(0, 15)], ag_s)
    sent(xb.at[0], agc_s)
    sent(r1_send, r1_s)

    result = hid_v[y] + r2_send[y, g].astype(F32)

    def add_from(s, first_g, count, total):
        def step(i, acc):
            return acc + r2_recv[s, (g + first_g + i) % 16].astype(F32)

        return lax.fori_loop(0, count, step, total, unroll=True)

    for j in range(3):
        s = (y + 3 - j) % 4
        taken(r2_recv.at[s], r2_r.at[s])
        result = add_from(s, 0, 16, result)
    taken(r2_recv.at[y, pl.ds(0, 15)], r2_r.at[y])
    result = add_from(y, 1, 15, result)
    mixed[...] = result.astype(BF16)
    sent(r2_send.at[pl.ds(0, 3)], r2_s.at[0])
    sent(r2_send.at[0, pl.ds(0, 15)], r2_s.at[1])


def finish(mixed_in, landed_in, mixed_out, landed_out, mixed_v, landed_v, sem):
    quarters = [pl.ds(4 * i, 4) for i in range(4)]
    into = [pltpu.make_async_copy(mixed_in, mixed_v, sem.at[4])] + [
        pltpu.make_async_copy(landed_in.at[q], landed_v.at[q], sem.at[i])
        for i, q in enumerate(quarters)
    ]
    out = [pltpu.make_async_copy(mixed_v, mixed_out, sem.at[4])] + [
        pltpu.make_async_copy(landed_v.at[q], landed_out.at[q], sem.at[i])
        for i, q in enumerate(quarters)
    ]
    for cp in into:
        cp.start()
    for first, then in zip(into, out):
        first.wait()
        then.start()
    for cp in out:
        cp.wait()


def body(
    queries,
    kv_cache,
    new_kv,
    lengths,
    residual,
    w_out,
    norm_gain,
    expert_ids,
    gate_w,
    w_inner,
    w_down,
    mig_rows,
    mig_dest,
):
    vmem = pltpu.VMEM
    dma = pltpu.SemaphoreType.DMA
    smem = pltpu.SMEM
    any_spec = pl.BlockSpec(memory_space=pl.ANY)
    vmem_spec = pl.BlockSpec(memory_space=pltpu.VMEM)
    mixed, landed = pl.pallas_call(
        kernel,
        out_shape=(
            jax.ShapeDtypeStruct((ROWS, BW), BF16),
            jax.ShapeDtypeStruct((16, PIECE, HD), BF16),
        ),
        in_specs=[any_spec] * 13,
        out_specs=(vmem_spec, any_spec),
        scratch_shapes=[
            smem((ROWS,), jnp.int32),
            smem((2, ROWS), jnp.int32),
            smem((2, ROWS), F32),
            smem((8,), jnp.int32),
            smem((8,), jnp.int32),
            vmem((HEADS, ROWS, HD), BF16),
            vmem((ROWS, 2 * SPAN, HD), BF16),
            vmem((ROWS, 2, HD), BF16),
            vmem((ROWS, BW), BF16),
            vmem((BW,), BF16),
            vmem((8, BW, BW), BF16),
            vmem((2 * D, HID), BF16),
            vmem((HID, D), BF16),
            vmem((16, PIECE, HD), BF16),
            vmem((16, PIECE, HD), BF16),
            vmem((16, PIECE, HD), BF16),
            vmem((16, ROWS, 128), F32),
            vmem((4, ROWS, BW), BF16),
            vmem((4, ROWS, BW), BF16),
            vmem((4, ROWS, BW), BF16),
            vmem((4, ROWS, BW), F32),
            vmem((4, ROWS, BW), BF16),
            vmem((4, 4, ROWS, BW), BF16),
            vmem((4, ROWS, BW), F32),
            vmem((2, ROWS, 128), F32),
            vmem((2, 4, 16, ROWS, BW), BF16),
            vmem((128, HID), BF16),
            vmem((256, HID), F32),
            vmem((4, 16, ROWS, BW), BF16),
            vmem((4, 16, ROWS, BW), BF16),
            vmem((4, 16, ROWS, BW), BF16),
            vmem((4, 16, ROWS, BW), BF16),
            dma((12,)),
            dma((8,)),
            dma,
            dma,
            dma,
            dma,
            dma,
            dma,
            dma,
            dma,
            dma,
            dma,
            dma((4,)),
            dma,
            dma((4,)),
            dma,
            dma,
            dma,
            dma((4,)),
            dma,
            dma((4,)),
            dma,
            dma((4,)),
            dma((2,)),
            dma((4,)),
            pltpu.SemaphoreType.REGULAR,
        ],
        compiler_params=pltpu.CompilerParams(
            collective_id=0,
            has_side_effects=True,
            vmem_limit_bytes=56 * 2**20,
        ),
        cost_estimate=pl.CostEstimate(
            flops=2 * (8 * BW * D + 256 * 2 * D * HID + 128 * HID * D),
            bytes_accessed=21 * 10**6,
            transcendentals=128 * HID,
        ),
    )(
        lengths,
        expert_ids.T,
        gate_w.T,
        mig_rows,
        mig_dest,
        queries.transpose(1, 0, 2),
        kv_cache.reshape(ROWS, 2 * SPAN, HD),
        new_kv.reshape(ROWS, 2, HD),
        residual,
        norm_gain,
        w_out,
        w_inner,
        w_down,
    )
    mixed, landed = pl.pallas_call(
        finish,
        out_shape=(
            jax.ShapeDtypeStruct((ROWS, BW), BF16),
            jax.ShapeDtypeStruct((16, PIECE, HD), BF16),
        ),
        in_specs=[any_spec] * 2,
        out_specs=(any_spec, any_spec),
        scratch_shapes=[
            vmem((ROWS, BW), BF16),
            vmem((16, PIECE, HD), BF16),
            dma((5,)),
        ],
        compiler_params=pltpu.CompilerParams(vmem_limit_bytes=56 * 2**20),
    )(mixed, landed)
    return mixed, landed.reshape(1, 2, 1, SPAN, HD)


def solution(mesh):
    in_specs = (
        P("grp", "tp", None),
        P("grp", None, "tp", None, None),
        P("grp", None, "tp", None),
        P("grp"),
        P("grp", "tp"),
        P("tp", None),
        P("tp"),
        P("grp", None),
        P("grp", None),
        P(None, None, ("grp", "tp")),
        P(("grp", "tp"), None),
        P(),
        P(),
    )
    out_specs = (P("grp", "tp"), P("grp", None, "tp", None, None))
    return jax.shard_map(body, mesh=mesh, in_specs=in_specs, out_specs=out_specs, check_vma=False)
```

```python
import functools

import jax
import jax.numpy as jnp
from jax import lax
from jax.experimental import pallas as pl
from jax.experimental.pallas import tpu as pltpu
from jax.sharding import PartitionSpec as P

MESH = pl.DeviceIdType.MESH
F32 = jnp.float32
BF16 = jnp.bfloat16
D = 6144
EXPERTS = 4
BW = 768
ROWS = 8
HEADS = 6
HD = 128
SPAN = 384
HID = 256
PIECE = 48


def remote(src, dst, send_sem, recv_sem, grp, tp):
    return pltpu.make_async_remote_copy(
        src_ref=src,
        dst_ref=dst,
        send_sem=send_sem,
        recv_sem=recv_sem,
        device_id=(grp, tp),
        device_id_type=MESH,
    )


def kernel(
    len_hbm,
    eids_hbm,
    gates_hbm,
    mrows_hbm,
    mdest_hbm,
    q_hbm,
    kv_hbm,
    new_hbm,
    res_hbm,
    gain_hbm,
    wo_hbm,
    wi_hbm,
    wd_hbm,
    mixed,
    landed,
    lengths,
    eids,
    gates,
    mrows,
    mdest,
    q_v,
    kv_v,
    new_v,
    res_v,
    gain_ref,
    wo_v,
    wi_v,
    wi2_v,
    wd_v,
    mig_out,
    mig_mid,
    mig_out2,
    gate_buf,
    gain_buf,
    sum_v,
    a_send,
    a_recv,
    hid_v,
    sq_buf,
    xb,
    act_v,
    acc_v,
    r1_send,
    r1_recv,
    r2_send,
    r2_recv,
    in_sem,
    wo_sem,
    loc_sem,
    mig_s,
    mig_r,
    mig2_s,
    mig2_r,
    gate_s,
    gate_r,
    gain_s,
    gain_r,
    a_s,
    a_r,
    sq_s,
    sq_r,
    ag_s,
    ag_r,
    agc_s,
    agc_r,
    r1_s,
    r1_r,
    r2_s,
    r2_r,
    ready,
):
    g = lax.axis_index("grp")
    t = lax.axis_index("tp")
    z, x = g // 4, g % 4
    y, c = t // 2, t % 2
    partner = y * 2 + 1 - c

    def taken(ref, sem):
        remote(ref, ref, sem, sem, g, t).wait_recv()

    def sent(ref, sem):
        remote(ref, ref, sem, sem, g, t).wait_send()

    ins = [
        pltpu.make_async_copy(kv_hbm, kv_v, in_sem.at[0]),
        pltpu.make_async_copy(q_hbm, q_v, in_sem.at[1]),
        pltpu.make_async_copy(new_hbm, new_v, in_sem.at[2]),
        pltpu.make_async_copy(res_hbm, res_v, in_sem.at[3]),
        pltpu.make_async_copy(len_hbm, lengths, in_sem.at[6]),
        pltpu.make_async_copy(eids_hbm, eids, in_sem.at[7]),
        pltpu.make_async_copy(gates_hbm, gates, in_sem.at[8]),
        pltpu.make_async_copy(mrows_hbm, mrows, in_sem.at[9]),
        pltpu.make_async_copy(mdest_hbm, mdest, in_sem.at[10]),
        pltpu.make_async_copy(gain_hbm, gain_ref, in_sem.at[11]),
    ]
    for cp in ins:
        cp.start()

    def wo_copy(i):
        b = (i // 2) * 2 + (c if i % 2 == 0 else 1 - c)
        return pltpu.make_async_copy(
            wo_hbm.at[:, pl.ds(pl.multiple_of(b * BW, BW), BW)], wo_v.at[i], wo_sem.at[i]
        )

    wi_cp = pltpu.make_async_copy(wi_hbm.reshape(2 * D, HID), wi_v, in_sem.at[4])
    wd_cp = pltpu.make_async_copy(wd_hbm, wd_v, in_sem.at[5])
    for i in range(3):
        wo_copy(i).start()

    barrier = pltpu.get_barrier_semaphore()

    def greet(sem, grp, tp):
        pl.semaphore_signal(sem, inc=1, device_id=(grp, tp), device_id_type=MESH)

    for d in range(1, 8):
        greet(barrier, g, (t + d) % 8)
    for d in range(1, 4):
        greet(barrier, (g + 4 * d) % 16, t)
        greet(barrier, z * 4 + (x + d) % 4, t)

    for cp in ins:
        cp.wait()
    wo_copy(3).start()
    qf = q_v[...].astype(F32).reshape(HEADS * ROWS, HD)
    qb = qf.astype(BF16)
    row_of = lax.broadcasted_iota(jnp.int32, (HEADS * ROWS, 1), 0) % ROWS
    scores = jnp.zeros((HEADS * ROWS, SPAN), F32)
    for r in range(ROWS):
        part = lax.dot_general(
            qb, kv_v[r, 0:SPAN, :], (((1,), (1,)), ((), ())), preferred_element_type=F32
        )
        scores = jnp.where(row_of == r, part, scores)
    wo_copy(4).start()
    scaling = HD ** (-0.5)
    scores = scores * scaling
    newf = new_v[...].astype(F32)
    new_k = jnp.concatenate([newf[:, 0, :]] * HEADS, axis=0)
    new_val = jnp.concatenate([newf[:, 1, :]] * HEADS, axis=0)
    own = jnp.sum(qf * new_k, axis=1, keepdims=True) * scaling
    span = jnp.zeros((HEADS * ROWS, 1), jnp.int32)
    for r in range(ROWS):
        span = jnp.where(row_of == r, lengths[r], span)
    seen = lax.broadcasted_iota(jnp.int32, (HEADS * ROWS, SPAN), 1) < span
    top = jnp.maximum(
        jnp.max(jnp.where(seen, scores, -jnp.inf), axis=1, keepdims=True), own
    )
    spread = jnp.where(seen, jnp.exp(scores - top), 0.0)
    own_exp = jnp.exp(own - top)
    denom = jnp.sum(spread, axis=1, keepdims=True) + own_exp
    weights = (spread / denom).astype(BF16)
    own_w = (own_exp / denom).astype(BF16).astype(F32)
    wo_copy(5).start()
    mix = jnp.zeros((HEADS * ROWS, HD), F32)
    for r in range(ROWS):
        part = jnp.dot(weights, kv_v[r, SPAN : 2 * SPAN, :], preferred_element_type=F32)
        mix = jnp.where(row_of == r, part, mix)
    mix = mix + own_w * new_val
    heads = jnp.concatenate(
        [mix[h * ROWS : (h + 1) * ROWS] for h in range(HEADS)], axis=1
    ).astype(BF16)
    wo_copy(6).start()
    wo_copy(7).start()
    wi_cp.start()
    wd_cp.start()

    row = jnp.int32(0)
    leaves = jnp.int32(0)
    for i in range(8):
        hit = (mrows[i] >> 3) == g
        row = row + jnp.where(hit, mrows[i] & 7, 0)
        leaves = leaves + jnp.where(hit, 1, 0)
    limit = jnp.int32(0)
    fresh_k = jnp.zeros((1, HD), F32)
    fresh_v = jnp.zeros((1, HD), F32)
    for r in range(ROWS):
        limit = limit + jnp.where(row == r, lengths[r], 0)
        fresh_k = jnp.where(row == r, new_k[r : r + 1], fresh_k)
        fresh_v = jnp.where(row == r, new_val[r : r + 1], fresh_v)
    limit = jnp.where(leaves > 0, limit, -1)

    def sealed(k):
        pos = lax.broadcasted_iota(jnp.int32, (PIECE, HD), 0) + (k % 8) * PIECE
        old = kv_v[row, pl.ds(pl.multiple_of(k * PIECE, PIECE), PIECE), :].astype(F32)
        fresh = jnp.where(k < 8, fresh_k, fresh_v)
        return jnp.where(
            pos < limit, old, jnp.where(pos == limit, fresh, 0.0)
        ).astype(BF16)

    def seal_step(k, _):
        mig_out[k] = sealed(k)
        return 0

    lax.fori_loop(0, 16, seal_step, 0)
    mig_mid[g] = mig_out[g]
    gain_buf[y] = gain_ref[...].astype(F32).reshape(1, BW)

    def a_copy(i, j, d):
        q = ((y + d) % 4) * 2 + (c if j == 0 else 1 - c)
        return remote(a_send.at[i, j], a_recv.at[i, t], a_s, a_r.at[i], g, q)

    def a_start(i):
        for j in range(2):
            for d in range(1 - j, 4):
                a_copy(i, j, d).start()

    def gain_copy(d):
        q = (y + d) % 4
        return remote(gain_buf.at[y], gain_buf.at[y], gain_s, gain_r, g, q * 2 + c)

    def mig_copy(i):
        k = (g + i) % 16
        return remote(mig_out.at[k], mig_mid.at[g], mig_s, mig_r, k, t)

    def project(i):
        wo_copy(2 * i).wait()
        part = jnp.dot(heads, wo_v[2 * i], preferred_element_type=F32)
        part = part + jnp.where(y == i, res_v[...].astype(F32), 0.0)
        sum_v[i] = part
        a_send[i, 0] = part.astype(BF16)
        wo_copy(2 * i + 1).wait()
        part = jnp.dot(heads, wo_v[2 * i + 1], preferred_element_type=F32)
        a_send[i, 1] = part.astype(BF16)

    project(0)
    project(1)
    pl.semaphore_wait(barrier, 13)
    a_start(0)
    for d in range(1, 4):
        greet(ready, z * 4 + (x + d) % 4, t)
    for d in range(1, 4):
        gain_copy(d).start()
    a_start(1)
    project(2)
    a_start(2)
    project(3)
    a_start(3)

    pl.semaphore_wait(ready, 3)

    @pl.loop(1, 16)
    def _(i):
        mig_copy(i).start()

    sub = lax.broadcasted_iota(jnp.int32, (ROWS, 128), 0)
    lane = lax.broadcasted_iota(jnp.int32, (ROWS, 128), 1)
    gate_rows = jnp.zeros((ROWS, 128), F32)
    for r in range(ROWS):
        for k in range(2):
            gate_rows = jnp.where(
                jnp.logical_and(sub == r, lane == eids[k, r]), gates[k, r], gate_rows
            )

    def ag_copy(i, d):
        return remote(
            xb.at[c, i, g], xb.at[c, i, g], ag_s, ag_r.at[i], (g + d) % 16, t
        )

    taken(gain_buf.at[pl.ds(0, 3)], gain_r)
    squares = jnp.zeros((ROWS, 1), F32)
    for i in range(4):
        taken(a_recv.at[i, pl.ds(0, 7)], a_r.at[i])
        hidden = sum_v[i]
        for d in range(1, 8):
            hidden = hidden + a_recv[i, (t + d) % 8].astype(F32)
        hid_v[i] = hidden
        squares = squares + jnp.sum(hidden * hidden, axis=1, keepdims=True)
        xb[c, i, g] = (hidden * gain_buf[i]).astype(BF16)

        @pl.loop(1, 16)
        def _(d):
            ag_copy(i, d).start()

    sq_buf[0] = jnp.broadcast_to(squares, (ROWS, 128))
    sq_copy = remote(sq_buf.at[0], sq_buf.at[1], sq_s, sq_r, g, partner)
    sq_copy.start()
    taken(sq_buf.at[1], sq_r)
    scale = lax.rsqrt((sq_buf[0] + sq_buf[1]) / D + 1e-05)
    gate_buf[g] = jnp.where(lane == EXPERTS, scale, gate_rows)

    def gate_copy(i):
        return remote(
            gate_buf.at[g], gate_buf.at[g], gate_s, gate_r, (g + i) % 16, t
        )

    @pl.loop(1, 16)
    def _(i):
        gate_copy(i).start()

    taken(mig_mid.at[pl.ds(0, 15)], mig_r)

    def mig2_copy(j):
        return remote(mig_out2.at[j], landed.at[g], mig2_s, mig2_r, j, t)

    def route_step(i, _):
        j = (g + i) % 16
        src = jnp.int32(0)
        some = jnp.int32(0)
        for k in range(8):
            hit = mdest[k] == j
            src = src + jnp.where(hit, mrows[k] >> 3, 0)
            some = some + jnp.where(hit, 1, 0)
        piece = mig_mid[src].astype(F32)
        mig_out2[j] = jnp.where(some > 0, piece, 0.0).astype(BF16)
        return 0

    lax.fori_loop(0, 16, route_step, 0)
    keep = pltpu.make_async_copy(mig_out2.at[g], landed.at[g], loc_sem)
    keep.start()

    sent(a_recv.at[:, pl.ds(0, 7)], a_s)
    sent(gain_buf.at[pl.ds(0, 3)], gain_s)
    sent(mig_out.at[pl.ds(0, 15)], mig_s)
    sent(sq_buf.at[0], sq_s)

    wi_cp.wait()
    ri = lax.broadcasted_iota(jnp.int32, (256, 256), 0)
    ci = lax.broadcasted_iota(jnp.int32, (256, 256), 1)
    spot = jnp.where(ri < 128, 2 * ri, 2 * ri - 255)
    apart = jnp.where(spot == ci, 1.0, 0.0).astype(BF16)

    def apart_step(k, _):
        pairs = wi_v[pl.ds(pl.multiple_of(k * 256, 256), 256), :]
        rows = jnp.dot(apart, pairs, preferred_element_type=F32).astype(BF16)
        at = pl.ds(pl.multiple_of(k * 128, 128), 128)
        wi2_v[at, 0:HID] = rows[0:128]
        wi2_v[at, HID : 2 * HID] = rows[128:256]
        return 0

    lax.fori_loop(0, D // 128, apart_step, 0, unroll=4)

    def agc_copy(i):
        return remote(xb.at[c, i], xb.at[c, i], agc_s, agc_r.at[i], g, partner)

    def up_part(h, yb):
        rows = jnp.concatenate(
            [xb[h, yb, k].astype(F32) for k in range(16)], axis=0
        )
        b = yb * 2 + h
        rhs = wi2_v[pl.ds(pl.multiple_of(b * BW, BW), BW), :]
        acc_v[...] += jnp.dot(rows.astype(BF16), rhs, preferred_element_type=F32)

    acc_v[...] = jnp.zeros_like(acc_v)

    def up_step(yb, _):
        @pl.when(yb < 4)
        def _():
            taken(xb.at[c, yb, pl.ds(0, 15)], ag_r.at[yb])
            agc_copy(yb).start()
            up_part(c, yb)

        @pl.when(yb == 4)
        def _():
            @pl.loop(1, 16)
            def _(i):
                mig2_copy((g + i) % 16).start()

        @pl.when(yb > 0)
        def _():
            taken(xb.at[1 - c, yb - 1], agc_r.at[yb - 1])
            up_part(1 - c, yb - 1)

        return 0

    lax.fori_loop(0, 5, up_step, 0)

    taken(gate_buf.at[pl.ds(0, 15)], gate_r)
    gate_all = jnp.concatenate([gate_buf[k] for k in range(16)], axis=0)
    expert = g // 4
    lane_all = lax.broadcasted_iota(jnp.int32, (128, 128), 1)
    gate_col = jnp.sum(
        jnp.where(lane_all == expert, gate_all, 0.0), axis=1, keepdims=True
    )
    scale_col = gate_all[:, EXPERTS : EXPERTS + 1]
    gate_part = acc_v[:, 0:HID] * scale_col
    up_value = acc_v[:, HID : 2 * HID] * scale_col
    silu = gate_part / (1.0 + jnp.exp(-gate_part))
    act_v[...] = (silu * up_value * gate_col).astype(BF16)

    wd_cp.wait()

    def down(h, yb):
        b = yb * 2 + h
        cols = pl.ds(pl.multiple_of(b * BW, BW), BW)
        return jnp.dot(act_v[...], wd_v[:, cols], preferred_element_type=F32)

    def r1_copy(yb):
        return remote(r1_send.at[yb], r1_recv.at[yb], r1_s, r1_r.at[yb], g, partner)

    def r1_step(j, _):
        yb = (y + 1 + j) % 4
        part = down(1 - c, yb)
        for k in range(16):
            r1_send[yb, k] = part[k * ROWS : (k + 1) * ROWS].astype(BF16)
        r1_copy(yb).start()
        return 0

    lax.fori_loop(0, 4, r1_step, 0)

    def r2_copy(j, yb, k):
        return remote(
            r2_send.at[yb, k], r2_recv.at[y, g], r2_s.at[j // 3], r2_r.at[y], k, yb * 2 + c
        )

    def r2_step(j, _):
        yb = (y + 1 + j) % 4
        part = down(c, yb)
        taken(r1_recv.at[yb], r1_r.at[yb])
        for k in range(16):
            both = part[k * ROWS : (k + 1) * ROWS] + r1_recv[yb, k].astype(F32)
            r2_send[yb, k] = both.astype(BF16)

        @pl.loop(1, 16)
        def _(i):
            r2_copy(j, yb, (g + i) % 16).start()

        @pl.when(j < 3)
        def _():
            r2_copy(j, yb, g).start()

        return 0

    lax.fori_loop(0, 4, r2_step, 0)

    keep.wait()
    taken(landed.at[pl.ds(0, 15)], mig2_r)
    sent(mig_out2.at[pl.ds(0, 15)], mig2_s)
    sent(gate_buf.at[pl.ds(0, 15)], gate_s)
    sent(xb.at[0, :, pl.ds(0, 15)], ag_s)
    sent(xb.at[0], agc_s)
    sent(r1_send, r1_s)

    result = hid_v[y] + r2_send[y, g].astype(F32)

    def add_from(s, first_g, count, total):
        def step(i, acc):
            return acc + r2_recv[s, (g + first_g + i) % 16].astype(F32)

        return lax.fori_loop(0, count, step, total, unroll=True)

    for j in range(3):
        s = (y + 3 - j) % 4
        taken(r2_recv.at[s], r2_r.at[s])
        result = add_from(s, 0, 16, result)
    taken(r2_recv.at[y, pl.ds(0, 15)], r2_r.at[y])
    result = add_from(y, 1, 15, result)
    mixed[...] = result.astype(BF16)
    sent(r2_send.at[pl.ds(0, 3)], r2_s.at[0])
    sent(r2_send.at[0, pl.ds(0, 15)], r2_s.at[1])


def finish(mixed_in, landed_in, mixed_out, landed_out, sem):
    cps = [
        pltpu.make_async_copy(mixed_in, mixed_out, sem.at[0]),
        pltpu.make_async_copy(landed_in, landed_out, sem.at[1]),
    ]
    for cp in cps:
        cp.start()
    for cp in cps:
        cp.wait()


def body(
    queries,
    kv_cache,
    new_kv,
    lengths,
    residual,
    w_out,
    norm_gain,
    expert_ids,
    gate_w,
    w_inner,
    w_down,
    mig_rows,
    mig_dest,
):
    vmem = pltpu.VMEM
    dma = pltpu.SemaphoreType.DMA
    smem = pltpu.SMEM
    any_spec = pl.BlockSpec(memory_space=pl.ANY)
    vmem_spec = pl.BlockSpec(memory_space=pltpu.VMEM)
    mixed, landed = pl.pallas_call(
        kernel,
        out_shape=(
            pltpu.VMEM((ROWS, BW), BF16),
            pltpu.VMEM((16, PIECE, HD), BF16),
        ),
        in_specs=[any_spec] * 13,
        out_specs=(vmem_spec, vmem_spec),
        scratch_shapes=[
            smem((ROWS,), jnp.int32),
            smem((2, ROWS), jnp.int32),
            smem((2, ROWS), F32),
            smem((8,), jnp.int32),
            smem((8,), jnp.int32),
            vmem((HEADS, ROWS, HD), BF16),
            vmem((ROWS, 2 * SPAN, HD), BF16),
            vmem((ROWS, 2, HD), BF16),
            vmem((ROWS, BW), BF16),
            vmem((BW,), BF16),
            vmem((8, BW, BW), BF16),
            vmem((2 * D, HID), BF16),
            vmem((D, 2 * HID), BF16),
            vmem((HID, D), BF16),
            vmem((16, PIECE, HD), BF16),
            vmem((16, PIECE, HD), BF16),
            vmem((16, PIECE, HD), BF16),
            vmem((16, ROWS, 128), F32),
            vmem((4, 1, BW), F32),
            vmem((4, ROWS, BW), F32),
            vmem((4, 2, ROWS, BW), BF16),
            vmem((4, 8, ROWS, BW), BF16),
            vmem((4, ROWS, BW), F32),
            vmem((2, ROWS, 128), F32),
            vmem((2, 4, 16, ROWS, BW), BF16),
            vmem((128, HID), BF16),
            vmem((128, 2 * HID), F32),
            vmem((4, 16, ROWS, BW), BF16),
            vmem((4, 16, ROWS, BW), BF16),
            vmem((4, 16, ROWS, BW), BF16),
            vmem((4, 16, ROWS, BW), BF16),
            dma((12,)),
            dma((8,)),
            dma,
            dma,
            dma,
            dma,
            dma,
            dma,
            dma,
            dma,
            dma,
            dma,
            dma((4,)),
            dma,
            dma,
            dma,
            dma((4,)),
            dma,
            dma((4,)),
            dma,
            dma((4,)),
            dma((2,)),
            dma((4,)),
            pltpu.SemaphoreType.REGULAR,
        ],
        compiler_params=pltpu.CompilerParams(
            collective_id=0,
            has_side_effects=True,
            vmem_limit_bytes=56 * 2**20,
        ),
        cost_estimate=pl.CostEstimate(
            flops=2 * (8 * BW * D + 256 * 2 * D * HID + 128 * HID * D),
            bytes_accessed=21 * 10**6,
            transcendentals=128 * HID,
        ),
    )(
        lengths,
        expert_ids.T,
        gate_w.T,
        mig_rows,
        mig_dest,
        queries.transpose(1, 0, 2),
        kv_cache.reshape(ROWS, 2 * SPAN, HD),
        new_kv.reshape(ROWS, 2, HD),
        residual,
        norm_gain,
        w_out,
        w_inner,
        w_down,
    )
    mixed, landed = pl.pallas_call(
        finish,
        out_shape=(
            jax.ShapeDtypeStruct((ROWS, BW), BF16),
            jax.ShapeDtypeStruct((16, PIECE, HD), BF16),
        ),
        in_specs=[vmem_spec] * 2,
        out_specs=(any_spec, any_spec),
        scratch_shapes=[dma((2,))],
        compiler_params=pltpu.CompilerParams(vmem_limit_bytes=56 * 2**20),
    )(
        pltpu.with_memory_space_constraint(mixed, pltpu.VMEM),
        pltpu.with_memory_space_constraint(landed, pltpu.VMEM),
    )
    return mixed, landed.reshape(1, 2, 1, SPAN, HD)


def solution(mesh):
    in_specs = (
        P("grp", "tp", None),
        P("grp", None, "tp", None, None),
        P("grp", None, "tp", None),
        P("grp"),
        P("grp", "tp"),
        P("tp", None),
        P("tp"),
        P("grp", None),
        P("grp", None),
        P(None, None, ("grp", "tp")),
        P(("grp", "tp"), None),
        P(),
        P(),
    )
    out_specs = (P("grp", "tp"), P("grp", None, "tp", None, None))
    return jax.shard_map(body, mesh=mesh, in_specs=in_specs, out_specs=out_specs, check_vma=False)
```

```python
import functools

import jax
import jax.numpy as jnp
from jax import lax
from jax.experimental import pallas as pl
from jax.experimental.pallas import tpu as pltpu
from jax.sharding import PartitionSpec as P

MESH = pl.DeviceIdType.MESH
F32 = jnp.float32
BF16 = jnp.bfloat16
D = 6144
EXPERTS = 4
BW = 768
ROWS = 8
HEADS = 6
HD = 128
SPAN = 384
HID = 256
FAR = [(2, 2), (2, 1), (2, 3), (1, 2), (3, 2)]
NEAR = [(1, 1), (1, 3), (3, 1), (3, 3), (2, 0), (0, 2), (1, 0), (3, 0), (0, 1), (0, 3)]
PIECE = 48


def remote(src, dst, send_sem, recv_sem, grp, tp):
    return pltpu.make_async_remote_copy(
        src_ref=src,
        dst_ref=dst,
        send_sem=send_sem,
        recv_sem=recv_sem,
        device_id=(grp, tp),
        device_id_type=MESH,
    )


def kernel(
    len_hbm,
    eids_hbm,
    gates_hbm,
    mrows_hbm,
    mdest_hbm,
    q_hbm,
    kv_hbm,
    new_hbm,
    res_hbm,
    gain_hbm,
    wo_hbm,
    wi_hbm,
    wd_hbm,
    mixed,
    landed,
    lengths,
    eids,
    gates,
    mrows,
    mdest,
    q_v,
    kv_v,
    new_v,
    res_v,
    gain_ref,
    wo_v,
    wi_v,
    wi2_v,
    wd_v,
    mig_out,
    mig_mid,
    mig_out2,
    gate_buf,
    a_send,
    a_recv,
    hid_v,
    sq_buf,
    xb,
    act_v,
    acc_v,
    r1_send,
    r1_recv,
    r2_send,
    r2_recv,
    in_sem,
    wo_sem,
    loc_sem,
    mig_s,
    mig_r,
    mig2_s,
    mig2_r,
    gate_s,
    gate_r,
    a_s,
    a_r,
    sq_s,
    sq_r,
    y_s,
    y_r,
    ag_s,
    ag_r,
    far_s,
    far_r,
    fwd_s,
    fwd_r,
    agc_s,
    agc_r,
    r1_s,
    r1_r,
    r2_s,
    r2_r,
    ready,
):
    g = lax.axis_index("grp")
    t = lax.axis_index("tp")
    z, x = g // 4, g % 4
    y, c = t // 2, t % 2
    partner = y * 2 + 1 - c

    def taken(ref, sem):
        remote(ref, ref, sem, sem, g, t).wait_recv()

    def sent(ref, sem):
        remote(ref, ref, sem, sem, g, t).wait_send()

    ins = [
        pltpu.make_async_copy(kv_hbm, kv_v, in_sem.at[0]),
        pltpu.make_async_copy(q_hbm, q_v, in_sem.at[1]),
        pltpu.make_async_copy(new_hbm, new_v, in_sem.at[2]),
        pltpu.make_async_copy(res_hbm, res_v, in_sem.at[3]),
        pltpu.make_async_copy(len_hbm, lengths, in_sem.at[6]),
        pltpu.make_async_copy(eids_hbm, eids, in_sem.at[7]),
        pltpu.make_async_copy(gates_hbm, gates, in_sem.at[8]),
        pltpu.make_async_copy(mrows_hbm, mrows, in_sem.at[9]),
        pltpu.make_async_copy(mdest_hbm, mdest, in_sem.at[10]),
        pltpu.make_async_copy(gain_hbm, gain_ref, in_sem.at[11]),
    ]
    for cp in ins:
        cp.start()

    def wo_copy(i):
        b = (t + 1 + i) % 8
        return pltpu.make_async_copy(
            wo_hbm.at[:, pl.ds(pl.multiple_of(b * BW, BW), BW)], wo_v.at[i], wo_sem.at[i]
        )

    wi_cp = pltpu.make_async_copy(wi_hbm.reshape(2 * D, HID), wi_v, in_sem.at[4])
    wd_cp = pltpu.make_async_copy(wd_hbm, wd_v, in_sem.at[5])
    for i in range(3):
        wo_copy(i).start()

    barrier = pltpu.get_barrier_semaphore()

    def greet(sem, grp, tp):
        pl.semaphore_signal(sem, inc=1, device_id=(grp, tp), device_id_type=MESH)

    for d in range(1, 8):
        greet(barrier, g, (t + d) % 8)
    for d in range(1, 4):
        greet(barrier, (g + 4 * d) % 16, t)
        greet(barrier, z * 4 + (x + d) % 4, t)

    for cp in ins:
        cp.wait()
    wo_copy(3).start()
    qf = q_v[...].astype(F32).reshape(HEADS * ROWS, HD)
    qb = qf.astype(BF16)
    row_of = lax.broadcasted_iota(jnp.int32, (HEADS * ROWS, 1), 0) % ROWS
    scores = jnp.zeros((HEADS * ROWS, SPAN), F32)
    for r in range(ROWS):
        part = lax.dot_general(
            qb, kv_v[r, 0:SPAN, :], (((1,), (1,)), ((), ())), preferred_element_type=F32
        )
        scores = jnp.where(row_of == r, part, scores)
    wo_copy(4).start()
    scaling = HD ** (-0.5)
    scores = scores * scaling
    newf = new_v[...].astype(F32)
    new_k = jnp.concatenate([newf[:, 0, :]] * HEADS, axis=0)
    new_val = jnp.concatenate([newf[:, 1, :]] * HEADS, axis=0)
    own = jnp.sum(qf * new_k, axis=1, keepdims=True) * scaling
    span = jnp.zeros((HEADS * ROWS, 1), jnp.int32)
    for r in range(ROWS):
        span = jnp.where(row_of == r, lengths[r], span)
    seen = lax.broadcasted_iota(jnp.int32, (HEADS * ROWS, SPAN), 1) < span
    top = jnp.maximum(
        jnp.max(jnp.where(seen, scores, -jnp.inf), axis=1, keepdims=True), own
    )
    spread = jnp.where(seen, jnp.exp(scores - top), 0.0)
    own_exp = jnp.exp(own - top)
    denom = jnp.sum(spread, axis=1, keepdims=True) + own_exp
    weights = (spread / denom).astype(BF16)
    own_w = (own_exp / denom).astype(BF16).astype(F32)
    wo_copy(5).start()
    mix = jnp.zeros((HEADS * ROWS, HD), F32)
    for r in range(ROWS):
        part = jnp.dot(weights, kv_v[r, SPAN : 2 * SPAN, :], preferred_element_type=F32)
        mix = jnp.where(row_of == r, part, mix)
    mix = mix + own_w * new_val
    heads = jnp.concatenate(
        [mix[h * ROWS : (h + 1) * ROWS] for h in range(HEADS)], axis=1
    ).astype(BF16)
    wo_copy(6).start()
    wo_copy(7).start()
    wi_cp.start()
    wd_cp.start()

    row = jnp.int32(0)
    leaves = jnp.int32(0)
    for i in range(8):
        hit = (mrows[i] >> 3) == g
        row = row + jnp.where(hit, mrows[i] & 7, 0)
        leaves = leaves + jnp.where(hit, 1, 0)
    limit = jnp.int32(0)
    fresh_k = jnp.zeros((1, HD), F32)
    fresh_v = jnp.zeros((1, HD), F32)
    for r in range(ROWS):
        limit = limit + jnp.where(row == r, lengths[r], 0)
        fresh_k = jnp.where(row == r, new_k[r : r + 1], fresh_k)
        fresh_v = jnp.where(row == r, new_val[r : r + 1], fresh_v)
    limit = jnp.where(leaves > 0, limit, -1)

    def sealed(k):
        pos = lax.broadcasted_iota(jnp.int32, (PIECE, HD), 0) + (k % 8) * PIECE
        old = kv_v[row, pl.ds(pl.multiple_of(k * PIECE, PIECE), PIECE), :].astype(F32)
        fresh = jnp.where(k < 8, fresh_k, fresh_v)
        return jnp.where(
            pos < limit, old, jnp.where(pos == limit, fresh, 0.0)
        ).astype(BF16)

    def seal_step(k, _):
        mig_out[k] = sealed(k)
        return 0

    lax.fori_loop(0, 16, seal_step, 0)
    mig_mid[g] = mig_out[g]

    def a_copy(i):
        return remote(a_send.at[i], a_recv.at[t], a_s, a_r, g, (t + 1 + i) % 8)

    def mig_copy(i):
        k = (g + i) % 16
        return remote(mig_out.at[k], mig_mid.at[g], mig_s, mig_r, k, t)

    def project(i):
        wo_copy(i).wait()
        return jnp.dot(heads, wo_v[i], preferred_element_type=F32)

    for i in range(6):
        a_send[i] = project(i).astype(BF16)
    pl.semaphore_wait(barrier, 13)
    for i in range(6):
        a_copy(i).start()
    for d in range(1, 4):
        greet(ready, z * 4 + (x + d) % 4, t)
    a_send[6] = project(6).astype(BF16)
    a_copy(6).start()
    hidden = res_v[...].astype(F32) + project(7)

    sub = lax.broadcasted_iota(jnp.int32, (ROWS, 128), 0)
    lane = lax.broadcasted_iota(jnp.int32, (ROWS, 128), 1)
    gate_rows = jnp.zeros((ROWS, 128), F32)
    for r in range(ROWS):
        for k in range(2):
            gate_rows = jnp.where(
                jnp.logical_and(sub == r, lane == eids[k, r]), gates[k, r], gate_rows
            )

    def plane(off):
        return ((z + off[0]) % 4) * 4 + (x + off[1]) % 4

    def y_copy(d):
        return remote(
            xb.at[c, y, g], xb.at[c, y, g], y_s, y_r.at[y], g, ((y + d) % 4) * 2 + c
        )

    def ag_copy(yb, off):
        return remote(
            xb.at[c, yb, g], xb.at[c, yb, g], ag_s, ag_r.at[yb], plane(off), t
        )

    def far_copy(off):
        return remote(xb.at[c, y, g], xb.at[c, y, g], far_s, far_r, plane(off), t)

    def fwd_copy(off, d):
        k = plane(off)
        return remote(
            xb.at[c, y, k],
            xb.at[c, y, k],
            fwd_s,
            fwd_r.at[y],
            g,
            ((y + d) % 4) * 2 + c,
        )

    def sq_copy(d):
        return remote(sq_buf.at[t], sq_buf.at[t], sq_s, sq_r, g, (t + d) % 8)

    pl.semaphore_wait(ready, 3)

    @pl.loop(1, 16)
    def _(i):
        mig_copy(i).start()

    wi_cp.wait()
    ri = lax.broadcasted_iota(jnp.int32, (256, 256), 0)
    ci = lax.broadcasted_iota(jnp.int32, (256, 256), 1)
    spot = jnp.where(ri < 128, 2 * ri, 2 * ri - 255)
    apart = jnp.where(spot == ci, 1.0, 0.0).astype(BF16)

    def apart_step(k, _):
        pairs = wi_v[pl.ds(pl.multiple_of(k * 256, 256), 256), :]
        rows = jnp.dot(apart, pairs, preferred_element_type=F32).astype(BF16)
        at = pl.ds(pl.multiple_of(k * 128, 128), 128)
        wi2_v[at, 0:HID] = rows[0:128]
        wi2_v[at, HID : 2 * HID] = rows[128:256]
        return 0

    lax.fori_loop(0, D // 256, apart_step, 0, unroll=4)

    taken(a_recv.at[pl.ds(0, 7)], a_r)
    for d in range(1, 8):
        hidden = hidden + a_recv[(t + d) % 8].astype(F32)
    hid_v[...] = hidden
    scaled = hidden * gain_ref[...].astype(F32).reshape(1, BW)
    xb[c, y, g] = scaled.astype(BF16)
    for d in range(1, 4):
        y_copy(d).start()
    for off in FAR:
        far_copy(off).start()
    for off in NEAR:
        ag_copy(y, off).start()
    squares = jnp.sum(hidden * hidden, axis=1, keepdims=True)
    sq_buf[t] = jnp.broadcast_to(squares, (ROWS, 128))
    for d in range(1, 8):
        sq_copy(d).start()

    lax.fori_loop(D // 256, D // 128, apart_step, 0, unroll=4)

    def pass_on(j, _):
        yb = (y + 4 - j) % 4
        taken(xb.at[c, yb, g], y_r.at[yb])
        for off in NEAR:
            ag_copy(yb, off).start()
        return 0

    lax.fori_loop(1, 4, pass_on, 0)

    taken(xb.at[c, y, pl.ds(0, 5)], far_r)
    for off in FAR:
        for d in range(1, 4):
            fwd_copy(off, d).start()

    taken(sq_buf.at[pl.ds(0, 7)], sq_r)
    total = sq_buf[0]
    for k in range(1, 8):
        total = total + sq_buf[k]
    scale = lax.rsqrt(total / D + 1e-05)
    gate_buf[g] = jnp.where(lane == EXPERTS, scale, gate_rows)

    def gate_copy(i):
        return remote(
            gate_buf.at[g], gate_buf.at[g], gate_s, gate_r, (g + i) % 16, t
        )

    @pl.loop(1, 16)
    def _(i):
        gate_copy(i).start()

    taken(mig_mid.at[pl.ds(0, 15)], mig_r)

    def mig2_copy(j):
        return remote(mig_out2.at[j], landed.at[g], mig2_s, mig2_r, j, t)

    def route_step(i, _):
        j = (g + i) % 16
        src = jnp.int32(0)
        some = jnp.int32(0)
        for k in range(8):
            hit = mdest[k] == j
            src = src + jnp.where(hit, mrows[k] >> 3, 0)
            some = some + jnp.where(hit, 1, 0)
        piece = mig_mid[src].astype(F32)
        mig_out2[j] = jnp.where(some > 0, piece, 0.0).astype(BF16)
        return 0

    lax.fori_loop(0, 16, route_step, 0)
    keep = pltpu.make_async_copy(mig_out2.at[g], landed.at[g], loc_sem)
    keep.start()

    @pl.loop(1, 16)
    def _(i):
        mig2_copy((g + i) % 16).start()


    sent(a_send, a_s)
    sent(mig_out.at[pl.ds(0, 15)], mig_s)
    sent(sq_buf.at[pl.ds(0, 7)], sq_s)

    def agc_copy(i):
        return remote(xb.at[c, i], xb.at[c, i], agc_s, agc_r.at[i], g, partner)

    def up_part(h, yb):
        rows = jnp.concatenate(
            [xb[h, yb, k].astype(F32) for k in range(16)], axis=0
        )
        b = yb * 2 + h
        rhs = wi2_v[pl.ds(pl.multiple_of(b * BW, BW), BW), :]
        acc_v[...] += jnp.dot(rows.astype(BF16), rhs, preferred_element_type=F32)

    acc_v[...] = jnp.zeros_like(acc_v)

    taken(xb.at[c, y, pl.ds(0, 10)], ag_r.at[y])
    agc_copy(y).start()
    up_part(c, y)
    taken(xb.at[1 - c, y], agc_r.at[y])
    up_part(1 - c, y)

    def arrive_step(j, _):
        yb = (y + 4 - j) % 4
        taken(xb.at[c, yb, pl.ds(0, 10)], ag_r.at[yb])
        taken(xb.at[c, yb, pl.ds(0, 5)], fwd_r.at[yb])
        agc_copy(yb).start()
        return 0

    lax.fori_loop(1, 4, arrive_step, 0)

    def own_step(j, _):
        up_part(c, (y + 4 - j) % 4)
        return 0

    lax.fori_loop(1, 4, own_step, 0)

    def other_step(j, _):
        yb = (y + 4 - j) % 4
        taken(xb.at[1 - c, yb], agc_r.at[yb])
        up_part(1 - c, yb)
        return 0

    lax.fori_loop(1, 4, other_step, 0)

    taken(gate_buf.at[pl.ds(0, 15)], gate_r)
    gate_all = jnp.concatenate([gate_buf[k] for k in range(16)], axis=0)
    expert = g // 4
    lane_all = lax.broadcasted_iota(jnp.int32, (128, 128), 1)
    gate_col = jnp.sum(
        jnp.where(lane_all == expert, gate_all, 0.0), axis=1, keepdims=True
    )
    scale_col = gate_all[:, EXPERTS : EXPERTS + 1]
    gate_part = acc_v[:, 0:HID] * scale_col
    up_value = acc_v[:, HID : 2 * HID] * scale_col
    silu = gate_part / (1.0 + jnp.exp(-gate_part))
    act_v[...] = (silu * up_value * gate_col).astype(BF16)

    wd_cp.wait()

    def down(h, yb):
        b = yb * 2 + h
        cols = pl.ds(pl.multiple_of(b * BW, BW), BW)
        return jnp.dot(act_v[...], wd_v[:, cols], preferred_element_type=F32)

    def r1_copy(yb):
        return remote(r1_send.at[yb], r1_recv.at[yb], r1_s, r1_r.at[yb], g, partner)

    def block_at(j):
        return (y + jnp.where(j == 0, 2, jnp.where(j == 1, 1, jnp.where(j == 2, 3, 0)))) % 4

    def r1_step(j, _):
        yb = block_at(j)
        part = down(1 - c, yb)
        for k in range(16):
            r1_send[yb, k] = part[k * ROWS : (k + 1) * ROWS].astype(BF16)
        r1_copy(yb).start()
        return 0

    lax.fori_loop(0, 4, r1_step, 0)

    def r2_copy(j, yb, k):
        return remote(
            r2_send.at[yb, k], r2_recv.at[y, g], r2_s.at[j // 3], r2_r.at[y], k, yb * 2 + c
        )

    def r2_step(j, _):
        yb = block_at(j)
        part = down(c, yb)
        taken(r1_recv.at[yb], r1_r.at[yb])
        for k in range(16):
            both = part[k * ROWS : (k + 1) * ROWS] + r1_recv[yb, k].astype(F32)
            r2_send[yb, k] = both.astype(BF16)

        for dz, dx in FAR + NEAR:
            r2_copy(j, yb, ((z + dz) % 4) * 4 + (x + dx) % 4).start()

        @pl.when(j < 3)
        def _():
            r2_copy(j, yb, g).start()

        return 0

    lax.fori_loop(0, 4, r2_step, 0)

    keep.wait()
    taken(landed.at[pl.ds(0, 15)], mig2_r)
    sent(mig_out2.at[pl.ds(0, 15)], mig2_s)
    sent(gate_buf.at[pl.ds(0, 15)], gate_s)
    sent(xb.at[0, 0, pl.ds(0, 3)], y_s)
    sent(xb.at[0, :, pl.ds(0, 10)], ag_s)
    sent(xb.at[0, 0, pl.ds(0, 5)], far_s)
    sent(xb.at[0, 0, pl.ds(0, 15)], fwd_s)
    sent(xb.at[0], agc_s)
    sent(r1_send, r1_s)

    result = hid_v[...] + r2_send[y, g].astype(F32)

    def add_from(s, first_g, count, total):
        def step(i, acc):
            return acc + r2_recv[s, (g + first_g + i) % 16].astype(F32)

        return lax.fori_loop(0, count, step, total, unroll=True)

    for j in (2, 3, 1):
        s = (y + j) % 4
        taken(r2_recv.at[s], r2_r.at[s])
        result = add_from(s, 0, 16, result)
    taken(r2_recv.at[y, pl.ds(0, 15)], r2_r.at[y])
    result = add_from(y, 1, 15, result)
    mixed[...] = result.astype(BF16)
    sent(r2_send.at[pl.ds(0, 3)], r2_s.at[0])
    sent(r2_send.at[0, pl.ds(0, 15)], r2_s.at[1])


def finish(mixed_in, landed_in, mixed_out, landed_out, sem):
    cps = [
        pltpu.make_async_copy(mixed_in, mixed_out, sem.at[0]),
        pltpu.make_async_copy(landed_in, landed_out, sem.at[1]),
    ]
    for cp in cps:
        cp.start()
    for cp in cps:
        cp.wait()


def body(
    queries,
    kv_cache,
    new_kv,
    lengths,
    residual,
    w_out,
    norm_gain,
    expert_ids,
    gate_w,
    w_inner,
    w_down,
    mig_rows,
    mig_dest,
):
    vmem = pltpu.VMEM
    dma = pltpu.SemaphoreType.DMA
    smem = pltpu.SMEM
    any_spec = pl.BlockSpec(memory_space=pl.ANY)
    vmem_spec = pl.BlockSpec(memory_space=pltpu.VMEM)
    mixed, landed = pl.pallas_call(
        kernel,
        out_shape=(
            pltpu.VMEM((ROWS, BW), BF16),
            pltpu.VMEM((16, PIECE, HD), BF16),
        ),
        in_specs=[any_spec] * 13,
        out_specs=(vmem_spec, vmem_spec),
        scratch_shapes=[
            smem((ROWS,), jnp.int32),
            smem((2, ROWS), jnp.int32),
            smem((2, ROWS), F32),
            smem((8,), jnp.int32),
            smem((8,), jnp.int32),
            vmem((HEADS, ROWS, HD), BF16),
            vmem((ROWS, 2 * SPAN, HD), BF16),
            vmem((ROWS, 2, HD), BF16),
            vmem((ROWS, BW), BF16),
            vmem((BW,), BF16),
            vmem((8, BW, BW), BF16),
            vmem((2 * D, HID), BF16),
            vmem((D, 2 * HID), BF16),
            vmem((HID, D), BF16),
            vmem((16, PIECE, HD), BF16),
            vmem((16, PIECE, HD), BF16),
            vmem((16, PIECE, HD), BF16),
            vmem((16, ROWS, 128), F32),
            vmem((7, ROWS, BW), BF16),
            vmem((8, ROWS, BW), BF16),
            vmem((ROWS, BW), F32),
            vmem((8, ROWS, 128), F32),
            vmem((2, 4, 16, ROWS, BW), BF16),
            vmem((128, HID), BF16),
            vmem((128, 2 * HID), F32),
            vmem((4, 16, ROWS, BW), BF16),
            vmem((4, 16, ROWS, BW), BF16),
            vmem((4, 16, ROWS, BW), BF16),
            vmem((4, 16, ROWS, BW), BF16),
            dma((12,)),
            dma((8,)),
            dma,
            dma,
            dma,
            dma,
            dma,
            dma,
            dma,
            dma,
            dma,
            dma,
            dma,
            dma,
            dma((4,)),
            dma,
            dma((4,)),
            dma,
            dma,
            dma,
            dma((4,)),
            dma,
            dma((4,)),
            dma,
            dma((4,)),
            dma((2,)),
            dma((4,)),
            pltpu.SemaphoreType.REGULAR,
        ],
        compiler_params=pltpu.CompilerParams(
            collective_id=0,
            has_side_effects=True,
            vmem_limit_bytes=56 * 2**20,
        ),
        cost_estimate=pl.CostEstimate(
            flops=2 * (8 * BW * D + 256 * 2 * D * HID + 128 * HID * D),
            bytes_accessed=21 * 10**6,
            transcendentals=128 * HID,
        ),
    )(
        lengths,
        expert_ids.T,
        gate_w.T,
        mig_rows,
        mig_dest,
        queries.transpose(1, 0, 2),
        kv_cache.reshape(ROWS, 2 * SPAN, HD),
        new_kv.reshape(ROWS, 2, HD),
        residual,
        norm_gain,
        w_out,
        w_inner,
        w_down,
    )
    mixed, landed = pl.pallas_call(
        finish,
        out_shape=(
            jax.ShapeDtypeStruct((ROWS, BW), BF16),
            jax.ShapeDtypeStruct((16, PIECE, HD), BF16),
        ),
        in_specs=[vmem_spec] * 2,
        out_specs=(any_spec, any_spec),
        scratch_shapes=[dma((2,))],
        compiler_params=pltpu.CompilerParams(vmem_limit_bytes=56 * 2**20),
    )(
        pltpu.with_memory_space_constraint(mixed, pltpu.VMEM),
        pltpu.with_memory_space_constraint(landed, pltpu.VMEM),
    )
    return mixed, landed.reshape(1, 2, 1, SPAN, HD)


def solution(mesh):
    in_specs = (
        P("grp", "tp", None),
        P("grp", None, "tp", None, None),
        P("grp", None, "tp", None),
        P("grp"),
        P("grp", "tp"),
        P("tp", None),
        P("tp"),
        P("grp", None),
        P("grp", None),
        P(None, None, ("grp", "tp")),
        P(("grp", "tp"), None),
        P(),
        P(),
    )
    out_specs = (P("grp", "tp"), P("grp", None, "tp", None, None))
    return jax.shard_map(body, mesh=mesh, in_specs=in_specs, out_specs=out_specs, check_vma=False)
```

```python
import functools

import jax
import jax.numpy as jnp
from jax import lax
from jax.experimental import pallas as pl
from jax.experimental.pallas import tpu as pltpu
from jax.sharding import PartitionSpec as P

MESH = pl.DeviceIdType.MESH
F32 = jnp.float32
BF16 = jnp.bfloat16
D = 6144
EXPERTS = 4
BW = 768
ROWS = 8
HEADS = 6
HD = 128
SPAN = 384
HID = 256
FAR = [(2, 2), (2, 1), (2, 3), (1, 2), (3, 2)]
NEAR = [(1, 1), (1, 3), (3, 1), (3, 3), (2, 0), (0, 2), (1, 0), (3, 0), (0, 1), (0, 3)]
PIECE = 48


def remote(src, dst, send_sem, recv_sem, grp, tp):
    return pltpu.make_async_remote_copy(
        src_ref=src,
        dst_ref=dst,
        send_sem=send_sem,
        recv_sem=recv_sem,
        device_id=(grp, tp),
        device_id_type=MESH,
    )


def kernel(
    len_hbm,
    eids_hbm,
    gates_hbm,
    mrows_hbm,
    mdest_hbm,
    q_hbm,
    kv_hbm,
    new_hbm,
    res_hbm,
    gain_hbm,
    wo_hbm,
    wi_hbm,
    wd_hbm,
    mixed,
    landed,
    lengths,
    eids,
    gates,
    mrows,
    mdest,
    q_v,
    kv_v,
    new_v,
    res_v,
    gain_ref,
    wo_v,
    wi_v,
    wi2_v,
    wd_v,
    mig_out,
    mig_mid,
    mig_out2,
    gate_buf,
    a_send,
    a_recv,
    hid_v,
    sq_buf,
    xb,
    act_v,
    acc_v,
    r1_send,
    r1_recv,
    r2_send,
    r2_recv,
    in_sem,
    wo_sem,
    loc_sem,
    mig_s,
    mig_r,
    mig2_s,
    mig2_r,
    gate_s,
    gate_r,
    a_s,
    a_r,
    sq_s,
    sq_r,
    y_s,
    y_r,
    ag_s,
    ag_r,
    far_s,
    far_r,
    fwd_s,
    fwd_r,
    agc_s,
    agc_r,
    r1_s,
    r1_r,
    r2_s,
    r2_r,
    ready,
):
    g = lax.axis_index("grp")
    t = lax.axis_index("tp")
    z, x = g // 4, g % 4
    y, c = t // 2, t % 2
    partner = y * 2 + 1 - c

    def taken(ref, sem):
        remote(ref, ref, sem, sem, g, t).wait_recv()

    def sent(ref, sem):
        remote(ref, ref, sem, sem, g, t).wait_send()

    ins = [
        pltpu.make_async_copy(kv_hbm, kv_v, in_sem.at[0]),
        pltpu.make_async_copy(q_hbm, q_v, in_sem.at[1]),
        pltpu.make_async_copy(new_hbm, new_v, in_sem.at[2]),
        pltpu.make_async_copy(res_hbm, res_v, in_sem.at[3]),
        pltpu.make_async_copy(len_hbm, lengths, in_sem.at[6]),
        pltpu.make_async_copy(eids_hbm, eids, in_sem.at[7]),
        pltpu.make_async_copy(gates_hbm, gates, in_sem.at[8]),
        pltpu.make_async_copy(mrows_hbm, mrows, in_sem.at[9]),
        pltpu.make_async_copy(mdest_hbm, mdest, in_sem.at[10]),
        pltpu.make_async_copy(gain_hbm, gain_ref, in_sem.at[11]),
    ]
    for cp in ins:
        cp.start()

    def wo_copy(i):
        b = (t + 1 + i) % 8
        return pltpu.make_async_copy(
            wo_hbm.at[:, pl.ds(pl.multiple_of(b * BW, BW), BW)], wo_v.at[i], wo_sem.at[i]
        )

    wi_cp = pltpu.make_async_copy(wi_hbm.reshape(2 * D, HID), wi_v, in_sem.at[4])
    wd_cp = pltpu.make_async_copy(wd_hbm, wd_v, in_sem.at[5])
    for i in range(3):
        wo_copy(i).start()

    barrier = pltpu.get_barrier_semaphore()

    def greet(sem, grp, tp):
        pl.semaphore_signal(sem, inc=1, device_id=(grp, tp), device_id_type=MESH)

    for d in range(1, 8):
        greet(barrier, g, (t + d) % 8)
    for d in range(1, 4):
        greet(barrier, (g + 4 * d) % 16, t)
        greet(barrier, z * 4 + (x + d) % 4, t)

    for cp in ins:
        cp.wait()
    wo_copy(3).start()
    qf = q_v[...].astype(F32).reshape(HEADS * ROWS, HD)
    qb = qf.astype(BF16)
    row_of = lax.broadcasted_iota(jnp.int32, (HEADS * ROWS, 1), 0) % ROWS
    scores = jnp.zeros((HEADS * ROWS, SPAN), F32)
    for r in range(ROWS):
        part = lax.dot_general(
            qb, kv_v[r, 0:SPAN, :], (((1,), (1,)), ((), ())), preferred_element_type=F32
        )
        scores = jnp.where(row_of == r, part, scores)
    wo_copy(4).start()
    scaling = HD ** (-0.5)
    scores = scores * scaling
    newf = new_v[...].astype(F32)
    new_k = jnp.concatenate([newf[:, 0, :]] * HEADS, axis=0)
    new_val = jnp.concatenate([newf[:, 1, :]] * HEADS, axis=0)
    own = jnp.sum(qf * new_k, axis=1, keepdims=True) * scaling
    span = jnp.zeros((HEADS * ROWS, 1), jnp.int32)
    for r in range(ROWS):
        span = jnp.where(row_of == r, lengths[r], span)
    seen = lax.broadcasted_iota(jnp.int32, (HEADS * ROWS, SPAN), 1) < span
    top = jnp.maximum(
        jnp.max(jnp.where(seen, scores, -jnp.inf), axis=1, keepdims=True), own
    )
    spread = jnp.where(seen, jnp.exp(scores - top), 0.0)
    own_exp = jnp.exp(own - top)
    denom = jnp.sum(spread, axis=1, keepdims=True) + own_exp
    weights = (spread / denom).astype(BF16)
    own_w = (own_exp / denom).astype(BF16).astype(F32)
    wo_copy(5).start()
    mix = jnp.zeros((HEADS * ROWS, HD), F32)
    for r in range(ROWS):
        part = jnp.dot(weights, kv_v[r, SPAN : 2 * SPAN, :], preferred_element_type=F32)
        mix = jnp.where(row_of == r, part, mix)
    mix = mix + own_w * new_val
    heads = jnp.concatenate(
        [mix[h * ROWS : (h + 1) * ROWS] for h in range(HEADS)], axis=1
    ).astype(BF16)
    wo_copy(6).start()
    wo_copy(7).start()
    wi_cp.start()
    wd_cp.start()

    row = jnp.int32(0)
    leaves = jnp.int32(0)
    for i in range(8):
        hit = (mrows[i] >> 3) == g
        row = row + jnp.where(hit, mrows[i] & 7, 0)
        leaves = leaves + jnp.where(hit, 1, 0)
    limit = jnp.int32(0)
    fresh_k = jnp.zeros((1, HD), F32)
    fresh_v = jnp.zeros((1, HD), F32)
    for r in range(ROWS):
        limit = limit + jnp.where(row == r, lengths[r], 0)
        fresh_k = jnp.where(row == r, new_k[r : r + 1], fresh_k)
        fresh_v = jnp.where(row == r, new_val[r : r + 1], fresh_v)
    limit = jnp.where(leaves > 0, limit, -1)

    def sealed(k):
        pos = lax.broadcasted_iota(jnp.int32, (PIECE, HD), 0) + (k % 8) * PIECE
        old = kv_v[row, pl.ds(pl.multiple_of(k * PIECE, PIECE), PIECE), :].astype(F32)
        fresh = jnp.where(k < 8, fresh_k, fresh_v)
        return jnp.where(
            pos < limit, old, jnp.where(pos == limit, fresh, 0.0)
        ).astype(BF16)

    def seal_step(k, _):
        mig_out[k] = sealed(k)
        return 0

    lax.fori_loop(0, 16, seal_step, 0)
    mig_mid[g] = mig_out[g]

    def a_copy(i):
        return remote(a_send.at[i], a_recv.at[t], a_s, a_r, g, (t + 1 + i) % 8)

    def mig_copy(i):
        k = (g + i) % 16
        return remote(mig_out.at[k], mig_mid.at[g], mig_s, mig_r, k, t)

    def project(i):
        wo_copy(i).wait()
        return jnp.dot(heads, wo_v[i], preferred_element_type=F32)

    for i in range(6):
        a_send[i] = project(i).astype(BF16)
    pl.semaphore_wait(barrier, 13)
    for i in range(6):
        a_copy(i).start()
    for d in range(1, 4):
        greet(ready, z * 4 + (x + d) % 4, t)
    a_send[6] = project(6).astype(BF16)
    a_copy(6).start()
    hidden = res_v[...].astype(F32) + project(7)

    sub = lax.broadcasted_iota(jnp.int32, (ROWS, 128), 0)
    lane = lax.broadcasted_iota(jnp.int32, (ROWS, 128), 1)
    gate_rows = jnp.zeros((ROWS, 128), F32)
    for r in range(ROWS):
        for k in range(2):
            gate_rows = jnp.where(
                jnp.logical_and(sub == r, lane == eids[k, r]), gates[k, r], gate_rows
            )

    def plane(off):
        return ((z + off[0]) % 4) * 4 + (x + off[1]) % 4

    def y_copy(d):
        return remote(
            xb.at[c, y, g], xb.at[c, y, g], y_s, y_r.at[y], g, ((y + d) % 4) * 2 + c
        )

    def ag_copy(yb, off):
        return remote(
            xb.at[c, yb, g], xb.at[c, yb, g], ag_s, ag_r.at[yb], plane(off), t
        )

    def far_copy(off):
        return remote(xb.at[c, y, g], xb.at[c, y, g], far_s, far_r, plane(off), t)

    def fwd_copy(off, d):
        k = plane(off)
        return remote(
            xb.at[c, y, k],
            xb.at[c, y, k],
            fwd_s,
            fwd_r.at[y],
            g,
            ((y + d) % 4) * 2 + c,
        )

    def sq_copy(d):
        return remote(sq_buf.at[t], sq_buf.at[t], sq_s, sq_r, g, (t + d) % 8)

    pl.semaphore_wait(ready, 3)

    @pl.loop(1, 16)
    def _(i):
        mig_copy(i).start()

    wi_cp.wait()
    ri = lax.broadcasted_iota(jnp.int32, (256, 256), 0)
    ci = lax.broadcasted_iota(jnp.int32, (256, 256), 1)
    spot = jnp.where(ri < 128, 2 * ri, 2 * ri - 255)
    apart = jnp.where(spot == ci, 1.0, 0.0).astype(BF16)

    def apart_step(k, _):
        pairs = wi_v[pl.ds(pl.multiple_of(k * 256, 256), 256), :]
        rows = jnp.dot(apart, pairs, preferred_element_type=F32).astype(BF16)
        at = pl.ds(pl.multiple_of(k * 128, 128), 128)
        wi2_v[at, 0:HID] = rows[0:128]
        wi2_v[at, HID : 2 * HID] = rows[128:256]
        return 0

    lax.fori_loop(0, 12, apart_step, 0, unroll=4)

    taken(a_recv.at[pl.ds(0, 7)], a_r)
    for d in range(1, 8):
        hidden = hidden + a_recv[(t + d) % 8].astype(F32)
    hid_v[...] = hidden
    scaled = hidden * gain_ref[...].astype(F32).reshape(1, BW)
    xb[c, y, g] = scaled.astype(BF16)
    for d in range(1, 4):
        y_copy(d).start()
    for off in FAR:
        far_copy(off).start()
    for off in NEAR:
        ag_copy(y, off).start()
    squares = jnp.sum(hidden * hidden, axis=1, keepdims=True)
    sq_buf[t] = jnp.broadcast_to(squares, (ROWS, 128))
    for d in range(1, 8):
        sq_copy(d).start()

    lax.fori_loop(12, 48, apart_step, 0, unroll=4)

    def pass_on(j, _):
        yb = (y + 4 - j) % 4
        taken(xb.at[c, yb, g], y_r.at[yb])
        for off in NEAR:
            ag_copy(yb, off).start()
        return 0

    lax.fori_loop(1, 4, pass_on, 0)

    taken(xb.at[c, y, pl.ds(0, 5)], far_r)
    for off in FAR:
        for d in range(1, 4):
            fwd_copy(off, d).start()

    taken(sq_buf.at[pl.ds(0, 7)], sq_r)
    total = sq_buf[0]
    for k in range(1, 8):
        total = total + sq_buf[k]
    scale = lax.rsqrt(total / D + 1e-05)
    gate_buf[g] = jnp.where(lane == EXPERTS, scale, gate_rows)

    def gate_copy(i):
        return remote(
            gate_buf.at[g], gate_buf.at[g], gate_s, gate_r, (g + i) % 16, t
        )

    @pl.loop(1, 16)
    def _(i):
        gate_copy(i).start()

    taken(mig_mid.at[pl.ds(0, 15)], mig_r)

    def mig2_copy(j):
        return remote(mig_out2.at[j], landed.at[g], mig2_s, mig2_r, j, t)

    def route_step(i, _):
        j = (g + i) % 16
        src = jnp.int32(0)
        some = jnp.int32(0)
        for k in range(8):
            hit = mdest[k] == j
            src = src + jnp.where(hit, mrows[k] >> 3, 0)
            some = some + jnp.where(hit, 1, 0)
        piece = mig_mid[src].astype(F32)
        mig_out2[j] = jnp.where(some > 0, piece, 0.0).astype(BF16)
        return 0

    lax.fori_loop(0, 16, route_step, 0)
    keep = pltpu.make_async_copy(mig_out2.at[g], landed.at[g], loc_sem)
    keep.start()

    @pl.loop(1, 16)
    def _(i):
        mig2_copy((g + i) % 16).start()


    sent(a_send, a_s)
    sent(mig_out.at[pl.ds(0, 15)], mig_s)
    sent(sq_buf.at[pl.ds(0, 7)], sq_s)

    def agc_copy(i):
        return remote(xb.at[c, i], xb.at[c, i], agc_s, agc_r.at[i], g, partner)

    def up_part(h, yb):
        rows = jnp.concatenate(
            [xb[h, yb, k].astype(F32) for k in range(16)], axis=0
        )
        b = yb * 2 + h
        rhs = wi2_v[pl.ds(pl.multiple_of(b * BW, BW), BW), :]
        acc_v[...] += jnp.dot(rows.astype(BF16), rhs, preferred_element_type=F32)

    acc_v[...] = jnp.zeros_like(acc_v)

    taken(xb.at[c, y, pl.ds(0, 10)], ag_r.at[y])
    agc_copy(y).start()
    up_part(c, y)
    taken(xb.at[1 - c, y], agc_r.at[y])
    up_part(1 - c, y)

    def arrive_step(j, _):
        yb = (y + 4 - j) % 4
        taken(xb.at[c, yb, pl.ds(0, 10)], ag_r.at[yb])
        taken(xb.at[c, yb, pl.ds(0, 5)], fwd_r.at[yb])
        agc_copy(yb).start()
        return 0

    lax.fori_loop(1, 4, arrive_step, 0)

    def own_step(j, _):
        up_part(c, (y + 4 - j) % 4)
        return 0

    lax.fori_loop(1, 4, own_step, 0, unroll=True)

    taken(gate_buf.at[pl.ds(0, 15)], gate_r)
    gate_all = jnp.concatenate([gate_buf[k] for k in range(16)], axis=0)
    expert = g // 4
    lane_all = lax.broadcasted_iota(jnp.int32, (128, 128), 1)
    gate_col = jnp.sum(
        jnp.where(lane_all == expert, gate_all, 0.0), axis=1, keepdims=True
    )
    scale_col = gate_all[:, EXPERTS : EXPERTS + 1]

    def other_step(j, _):
        yb = (y + 4 - j) % 4
        taken(xb.at[1 - c, yb], agc_r.at[yb])
        up_part(1 - c, yb)
        return 0

    lax.fori_loop(1, 4, other_step, 0)

    gate_part = acc_v[:, 0:HID] * scale_col
    up_value = acc_v[:, HID : 2 * HID] * scale_col
    silu = gate_part / (1.0 + jnp.exp(-gate_part))
    act_v[...] = (silu * up_value * gate_col).astype(BF16)

    wd_cp.wait()

    def down(h, yb):
        b = yb * 2 + h
        cols = pl.ds(pl.multiple_of(b * BW, BW), BW)
        return jnp.dot(act_v[...], wd_v[:, cols], preferred_element_type=F32)

    def r1_copy(yb):
        return remote(r1_send.at[yb], r1_recv.at[yb], r1_s, r1_r.at[yb], g, partner)

    def block_at(j):
        return (y + jnp.where(j == 0, 2, jnp.where(j == 1, 1, jnp.where(j == 2, 3, 0)))) % 4

    def r1_step(j, _):
        yb = block_at(j)
        part = down(1 - c, yb)
        for k in range(16):
            r1_send[yb, k] = part[k * ROWS : (k + 1) * ROWS].astype(BF16)
        r1_copy(yb).start()
        return 0

    lax.fori_loop(0, 4, r1_step, 0, unroll=True)

    def r2_copy(j, yb, k):
        return remote(
            r2_send.at[yb, k], r2_recv.at[y, g], r2_s.at[j // 3], r2_r.at[y], k, yb * 2 + c
        )

    def r2_step(j, _):
        yb = block_at(j)
        part = down(c, yb)
        taken(r1_recv.at[yb], r1_r.at[yb])
        for k in range(16):
            both = part[k * ROWS : (k + 1) * ROWS] + r1_recv[yb, k].astype(F32)
            r2_send[yb, k] = both.astype(BF16)

        for dz, dx in FAR + NEAR:
            r2_copy(j, yb, ((z + dz) % 4) * 4 + (x + dx) % 4).start()

        @pl.when(j < 3)
        def _():
            r2_copy(j, yb, g).start()

        return 0

    lax.fori_loop(0, 4, r2_step, 0)

    keep.wait()
    taken(landed.at[pl.ds(0, 15)], mig2_r)
    sent(mig_out2.at[pl.ds(0, 15)], mig2_s)
    sent(gate_buf.at[pl.ds(0, 15)], gate_s)
    sent(xb.at[0, 0, pl.ds(0, 3)], y_s)
    sent(xb.at[0, :, pl.ds(0, 10)], ag_s)
    sent(xb.at[0, 0, pl.ds(0, 5)], far_s)
    sent(xb.at[0, 0, pl.ds(0, 15)], fwd_s)
    sent(xb.at[0], agc_s)
    sent(r1_send, r1_s)

    result = hid_v[...] + r2_send[y, g].astype(F32)

    def add_from(s, first_g, count, total):
        def step(i, acc):
            return acc + r2_recv[s, (g + first_g + i) % 16].astype(F32)

        return lax.fori_loop(0, count, step, total, unroll=True)

    for j in (2, 3, 1):
        s = (y + j) % 4
        taken(r2_recv.at[s], r2_r.at[s])
        result = add_from(s, 0, 16, result)
    taken(r2_recv.at[y, pl.ds(0, 15)], r2_r.at[y])
    result = add_from(y, 1, 15, result)
    mixed[...] = result.astype(BF16)
    sent(r2_send.at[pl.ds(0, 3)], r2_s.at[0])
    sent(r2_send.at[0, pl.ds(0, 15)], r2_s.at[1])


def finish(mixed_in, landed_in, mixed_out, landed_out, sem):
    cps = [
        pltpu.make_async_copy(mixed_in, mixed_out, sem.at[0]),
        pltpu.make_async_copy(landed_in, landed_out, sem.at[1]),
    ]
    for cp in cps:
        cp.start()
    for cp in cps:
        cp.wait()


def body(
    queries,
    kv_cache,
    new_kv,
    lengths,
    residual,
    w_out,
    norm_gain,
    expert_ids,
    gate_w,
    w_inner,
    w_down,
    mig_rows,
    mig_dest,
):
    vmem = pltpu.VMEM
    dma = pltpu.SemaphoreType.DMA
    smem = pltpu.SMEM
    any_spec = pl.BlockSpec(memory_space=pl.ANY)
    vmem_spec = pl.BlockSpec(memory_space=pltpu.VMEM)
    mixed, landed = pl.pallas_call(
        kernel,
        out_shape=(
            pltpu.VMEM((ROWS, BW), BF16),
            pltpu.VMEM((16, PIECE, HD), BF16),
        ),
        in_specs=[any_spec] * 13,
        out_specs=(vmem_spec, vmem_spec),
        scratch_shapes=[
            smem((ROWS,), jnp.int32),
            smem((2, ROWS), jnp.int32),
            smem((2, ROWS), F32),
            smem((8,), jnp.int32),
            smem((8,), jnp.int32),
            vmem((HEADS, ROWS, HD), BF16),
            vmem((ROWS, 2 * SPAN, HD), BF16),
            vmem((ROWS, 2, HD), BF16),
            vmem((ROWS, BW), BF16),
            vmem((BW,), BF16),
            vmem((8, BW, BW), BF16),
            vmem((2 * D, HID), BF16),
            vmem((D, 2 * HID), BF16),
            vmem((HID, D), BF16),
            vmem((16, PIECE, HD), BF16),
            vmem((16, PIECE, HD), BF16),
            vmem((16, PIECE, HD), BF16),
            vmem((16, ROWS, 128), F32),
            vmem((7, ROWS, BW), BF16),
            vmem((8, ROWS, BW), BF16),
            vmem((ROWS, BW), F32),
            vmem((8, ROWS, 128), F32),
            vmem((2, 4, 16, ROWS, BW), BF16),
            vmem((128, HID), BF16),
            vmem((128, 2 * HID), F32),
            vmem((4, 16, ROWS, BW), BF16),
            vmem((4, 16, ROWS, BW), BF16),
            vmem((4, 16, ROWS, BW), BF16),
            vmem((4, 16, ROWS, BW), BF16),
            dma((12,)),
            dma((8,)),
            dma,
            dma,
            dma,
            dma,
            dma,
            dma,
            dma,
            dma,
            dma,
            dma,
            dma,
            dma,
            dma((4,)),
            dma,
            dma((4,)),
            dma,
            dma,
            dma,
            dma((4,)),
            dma,
            dma((4,)),
            dma,
            dma((4,)),
            dma((2,)),
            dma((4,)),
            pltpu.SemaphoreType.REGULAR,
        ],
        compiler_params=pltpu.CompilerParams(
            collective_id=0,
            has_side_effects=True,
            vmem_limit_bytes=56 * 2**20,
        ),
        cost_estimate=pl.CostEstimate(
            flops=2 * (8 * BW * D + 256 * 2 * D * HID + 128 * HID * D),
            bytes_accessed=21 * 10**6,
            transcendentals=128 * HID,
        ),
    )(
        lengths,
        expert_ids.T,
        gate_w.T,
        mig_rows,
        mig_dest,
        queries.transpose(1, 0, 2),
        kv_cache.reshape(ROWS, 2 * SPAN, HD),
        new_kv.reshape(ROWS, 2, HD),
        residual,
        norm_gain,
        w_out,
        w_inner,
        w_down,
    )
    mixed, landed = pl.pallas_call(
        finish,
        out_shape=(
            jax.ShapeDtypeStruct((ROWS, BW), BF16),
            jax.ShapeDtypeStruct((16, PIECE, HD), BF16),
        ),
        in_specs=[vmem_spec] * 2,
        out_specs=(any_spec, any_spec),
        scratch_shapes=[dma((2,))],
        compiler_params=pltpu.CompilerParams(vmem_limit_bytes=56 * 2**20),
    )(
        pltpu.with_memory_space_constraint(mixed, pltpu.VMEM),
        pltpu.with_memory_space_constraint(landed, pltpu.VMEM),
    )
    return mixed, landed.reshape(1, 2, 1, SPAN, HD)


def solution(mesh):
    in_specs = (
        P("grp", "tp", None),
        P("grp", None, "tp", None, None),
        P("grp", None, "tp", None),
        P("grp"),
        P("grp", "tp"),
        P("tp", None),
        P("tp"),
        P("grp", None),
        P("grp", None),
        P(None, None, ("grp", "tp")),
        P(("grp", "tp"), None),
        P(),
        P(),
    )
    out_specs = (P("grp", "tp"), P("grp", None, "tp", None, None))
    return jax.shard_map(body, mesh=mesh, in_specs=in_specs, out_specs=out_specs, check_vma=False)
```

```python
import functools

import jax
import jax.numpy as jnp
from jax import lax
from jax.experimental import pallas as pl
from jax.experimental.pallas import tpu as pltpu
from jax.sharding import PartitionSpec as P

MESH = pl.DeviceIdType.MESH
F32 = jnp.float32
BF16 = jnp.bfloat16
D = 6144
EXPERTS = 4
BW = 768
ROWS = 8
HEADS = 6
HD = 128
SPAN = 384
HID = 256
FAR = [(2, 2), (2, 1), (2, 3), (1, 2), (3, 2)]
NEAR = [(1, 1), (1, 3), (3, 1), (3, 3), (2, 0), (0, 2), (1, 0), (3, 0), (0, 1), (0, 3)]
PIECE = 48


def remote(src, dst, send_sem, recv_sem, grp, tp):
    return pltpu.make_async_remote_copy(
        src_ref=src,
        dst_ref=dst,
        send_sem=send_sem,
        recv_sem=recv_sem,
        device_id=(grp, tp),
        device_id_type=MESH,
    )


def kernel(
    len_hbm,
    eids_hbm,
    gates_hbm,
    mrows_hbm,
    mdest_hbm,
    q_hbm,
    kv_hbm,
    new_hbm,
    res_hbm,
    gain_hbm,
    wo_hbm,
    wi_hbm,
    wd_hbm,
    mixed,
    landed,
    lengths,
    eids,
    gates,
    mrows,
    mdest,
    q_v,
    kv_v,
    new_v,
    res_v,
    gain_ref,
    wo_v,
    wi_v,
    wi2_v,
    wd_v,
    mig_out,
    mig_mid,
    mig_out2,
    gate_buf,
    a_send,
    a_recv,
    hid_v,
    sq_buf,
    xb,
    act_v,
    acc_v,
    part_v,
    r1_send,
    r1_recv,
    r2_send,
    r2_recv,
    in_sem,
    wo_sem,
    loc_sem,
    mig_s,
    mig_r,
    mig2_s,
    mig2_r,
    gate_s,
    gate_r,
    a_s,
    a_r,
    sq_s,
    sq_r,
    y_s,
    y_r,
    ag_s,
    ag_r,
    far_s,
    far_r,
    fwd_s,
    fwd_r,
    agc_s,
    agc_r,
    r1_s,
    r1_r,
    r2_s,
    r2_r,
    ready,
):
    g = lax.axis_index("grp")
    t = lax.axis_index("tp")
    z, x = g // 4, g % 4
    y, c = t // 2, t % 2
    partner = y * 2 + 1 - c

    def taken(ref, sem):
        remote(ref, ref, sem, sem, g, t).wait_recv()

    def sent(ref, sem):
        remote(ref, ref, sem, sem, g, t).wait_send()

    ins = [
        pltpu.make_async_copy(kv_hbm, kv_v, in_sem.at[0]),
        pltpu.make_async_copy(q_hbm, q_v, in_sem.at[1]),
        pltpu.make_async_copy(new_hbm, new_v, in_sem.at[2]),
        pltpu.make_async_copy(res_hbm, res_v, in_sem.at[3]),
        pltpu.make_async_copy(len_hbm, lengths, in_sem.at[6]),
        pltpu.make_async_copy(eids_hbm, eids, in_sem.at[7]),
        pltpu.make_async_copy(gates_hbm, gates, in_sem.at[8]),
        pltpu.make_async_copy(mrows_hbm, mrows, in_sem.at[9]),
        pltpu.make_async_copy(mdest_hbm, mdest, in_sem.at[10]),
        pltpu.make_async_copy(gain_hbm, gain_ref, in_sem.at[11]),
    ]
    for cp in ins:
        cp.start()

    def wo_copy(i):
        b = (t + 1 + i) % 8
        return pltpu.make_async_copy(
            wo_hbm.at[:, pl.ds(pl.multiple_of(b * BW, BW), BW)], wo_v.at[i], wo_sem.at[i]
        )

    wi_cp = pltpu.make_async_copy(wi_hbm.reshape(2 * D, HID), wi_v, in_sem.at[4])
    wd_cp = pltpu.make_async_copy(wd_hbm, wd_v, in_sem.at[5])
    for i in range(3):
        wo_copy(i).start()

    barrier = pltpu.get_barrier_semaphore()

    def greet(sem, grp, tp):
        pl.semaphore_signal(sem, inc=1, device_id=(grp, tp), device_id_type=MESH)

    for d in range(1, 8):
        greet(barrier, g, (t + d) % 8)
    for d in range(1, 4):
        greet(barrier, (g + 4 * d) % 16, t)
        greet(barrier, z * 4 + (x + d) % 4, t)

    for cp in ins:
        cp.wait()
    wo_copy(3).start()
    qf = q_v[...].astype(F32).reshape(HEADS * ROWS, HD)
    qb = qf.astype(BF16)
    row_of = lax.broadcasted_iota(jnp.int32, (HEADS * ROWS, 1), 0) % ROWS
    scores = jnp.zeros((HEADS * ROWS, SPAN), F32)
    for r in range(ROWS):
        part = lax.dot_general(
            qb, kv_v[r, 0:SPAN, :], (((1,), (1,)), ((), ())), preferred_element_type=F32
        )
        scores = jnp.where(row_of == r, part, scores)
    wo_copy(4).start()
    scaling = HD ** (-0.5)
    scores = scores * scaling
    newf = new_v[...].astype(F32)
    new_k = jnp.concatenate([newf[:, 0, :]] * HEADS, axis=0)
    new_val = jnp.concatenate([newf[:, 1, :]] * HEADS, axis=0)
    own = jnp.sum(qf * new_k, axis=1, keepdims=True) * scaling
    span = jnp.zeros((HEADS * ROWS, 1), jnp.int32)
    for r in range(ROWS):
        span = jnp.where(row_of == r, lengths[r], span)
    seen = lax.broadcasted_iota(jnp.int32, (HEADS * ROWS, SPAN), 1) < span
    top = jnp.maximum(
        jnp.max(jnp.where(seen, scores, -jnp.inf), axis=1, keepdims=True), own
    )
    spread = jnp.where(seen, jnp.exp(scores - top), 0.0)
    own_exp = jnp.exp(own - top)
    denom = jnp.sum(spread, axis=1, keepdims=True) + own_exp
    weights = (spread / denom).astype(BF16)
    own_w = (own_exp / denom).astype(BF16).astype(F32)
    wo_copy(5).start()
    mix = jnp.zeros((HEADS * ROWS, HD), F32)
    for r in range(ROWS):
        part = jnp.dot(weights, kv_v[r, SPAN : 2 * SPAN, :], preferred_element_type=F32)
        mix = jnp.where(row_of == r, part, mix)
    mix = mix + own_w * new_val
    heads = jnp.concatenate(
        [mix[h * ROWS : (h + 1) * ROWS] for h in range(HEADS)], axis=1
    ).astype(BF16)
    wo_copy(6).start()
    wo_copy(7).start()
    wi_cp.start()
    wd_cp.start()

    row = jnp.int32(0)
    leaves = jnp.int32(0)
    for i in range(8):
        hit = (mrows[i] >> 3) == g
        row = row + jnp.where(hit, mrows[i] & 7, 0)
        leaves = leaves + jnp.where(hit, 1, 0)
    limit = jnp.int32(0)
    fresh_k = jnp.zeros((1, HD), F32)
    fresh_v = jnp.zeros((1, HD), F32)
    for r in range(ROWS):
        limit = limit + jnp.where(row == r, lengths[r], 0)
        fresh_k = jnp.where(row == r, new_k[r : r + 1], fresh_k)
        fresh_v = jnp.where(row == r, new_val[r : r + 1], fresh_v)
    limit = jnp.where(leaves > 0, limit, -1)

    def sealed(k):
        pos = lax.broadcasted_iota(jnp.int32, (PIECE, HD), 0) + (k % 8) * PIECE
        old = kv_v[row, pl.ds(pl.multiple_of(k * PIECE, PIECE), PIECE), :].astype(F32)
        fresh = jnp.where(k < 8, fresh_k, fresh_v)
        return jnp.where(
            pos < limit, old, jnp.where(pos == limit, fresh, 0.0)
        ).astype(BF16)

    def seal_step(k, _):
        mig_out[k] = sealed(k)
        return 0

    lax.fori_loop(0, 16, seal_step, 0)
    mig_mid[g] = mig_out[g]

    def a_copy(i):
        return remote(a_send.at[i], a_recv.at[t], a_s, a_r, g, (t + 1 + i) % 8)

    def mig_copy(i):
        k = (g + i) % 16
        return remote(mig_out.at[k], mig_mid.at[g], mig_s, mig_r, k, t)

    def project(i):
        wo_copy(i).wait()
        return jnp.dot(heads, wo_v[i], preferred_element_type=F32)

    for i in range(6):
        a_send[i] = project(i).astype(BF16)
    pl.semaphore_wait(barrier, 13)
    for i in range(6):
        a_copy(i).start()
    for d in range(1, 4):
        greet(ready, z * 4 + (x + d) % 4, t)
    a_send[6] = project(6).astype(BF16)
    a_copy(6).start()
    hidden = res_v[...].astype(F32) + project(7)

    sub = lax.broadcasted_iota(jnp.int32, (ROWS, 128), 0)
    lane = lax.broadcasted_iota(jnp.int32, (ROWS, 128), 1)
    gate_rows = jnp.zeros((ROWS, 128), F32)
    for r in range(ROWS):
        for k in range(2):
            gate_rows = jnp.where(
                jnp.logical_and(sub == r, lane == eids[k, r]), gates[k, r], gate_rows
            )

    def plane(off):
        return ((z + off[0]) % 4) * 4 + (x + off[1]) % 4

    def y_copy(d):
        return remote(
            xb.at[c, y, g], xb.at[c, y, g], y_s, y_r.at[y], g, ((y + d) % 4) * 2 + c
        )

    def ag_copy(yb, off):
        return remote(
            xb.at[c, yb, g], xb.at[c, yb, g], ag_s, ag_r.at[yb], plane(off), t
        )

    def far_copy(off):
        return remote(xb.at[c, y, g], xb.at[c, y, g], far_s, far_r, plane(off), t)

    def fwd_copy(off, d):
        k = plane(off)
        return remote(
            xb.at[c, y, k],
            xb.at[c, y, k],
            fwd_s,
            fwd_r.at[y],
            g,
            ((y + d) % 4) * 2 + c,
        )

    def sq_copy(d):
        return remote(sq_buf.at[t], sq_buf.at[t], sq_s, sq_r, g, (t + d) % 8)

    pl.semaphore_wait(ready, 3)

    @pl.loop(1, 16)
    def _(i):
        mig_copy(i).start()

    wi_cp.wait()
    ri = lax.broadcasted_iota(jnp.int32, (256, 256), 0)
    ci = lax.broadcasted_iota(jnp.int32, (256, 256), 1)
    spot = jnp.where(ri < 128, 2 * ri, 2 * ri - 255)
    apart = jnp.where(spot == ci, 1.0, 0.0).astype(BF16)

    def apart_step(k, _):
        pairs = wi_v[pl.ds(pl.multiple_of(k * 256, 256), 256), :]
        rows = jnp.dot(apart, pairs, preferred_element_type=F32).astype(BF16)
        at = pl.ds(pl.multiple_of(k * 128, 128), 128)
        wi2_v[at, 0:HID] = rows[0:128]
        wi2_v[at, HID : 2 * HID] = rows[128:256]
        return 0

    lax.fori_loop(0, 12, apart_step, 0, unroll=4)

    taken(a_recv.at[pl.ds(0, 7)], a_r)
    for d in range(1, 8):
        hidden = hidden + a_recv[(t + d) % 8].astype(F32)
    hid_v[...] = hidden
    scaled = hidden * gain_ref[...].astype(F32).reshape(1, BW)
    xb[c, y, g] = scaled.astype(BF16)
    for d in range(1, 4):
        y_copy(d).start()
    for off in FAR:
        far_copy(off).start()
    for off in NEAR:
        ag_copy(y, off).start()
    squares = jnp.sum(hidden * hidden, axis=1, keepdims=True)
    sq_buf[t] = jnp.broadcast_to(squares, (ROWS, 128))
    for d in range(1, 8):
        sq_copy(d).start()

    lax.fori_loop(12, 48, apart_step, 0, unroll=4)

    def pass_on(j, _):
        yb = (y + 4 - j) % 4
        taken(xb.at[c, yb, g], y_r.at[yb])
        for off in NEAR:
            ag_copy(yb, off).start()
        return 0

    lax.fori_loop(1, 4, pass_on, 0)

    taken(xb.at[c, y, pl.ds(0, 5)], far_r)
    for off in FAR:
        for d in range(1, 4):
            fwd_copy(off, d).start()

    taken(sq_buf.at[pl.ds(0, 7)], sq_r)
    total = sq_buf[0]
    for k in range(1, 8):
        total = total + sq_buf[k]
    scale = lax.rsqrt(total / D + 1e-05)
    gate_buf[g] = jnp.where(lane == EXPERTS, scale, gate_rows)

    def gate_copy(i):
        return remote(
            gate_buf.at[g], gate_buf.at[g], gate_s, gate_r, (g + i) % 16, t
        )

    @pl.loop(1, 16)
    def _(i):
        gate_copy(i).start()

    taken(mig_mid.at[pl.ds(0, 15)], mig_r)

    def mig2_copy(j):
        return remote(mig_out2.at[j], landed.at[g], mig2_s, mig2_r, j, t)

    def route_step(i, _):
        j = (g + i) % 16
        src = jnp.int32(0)
        some = jnp.int32(0)
        for k in range(8):
            hit = mdest[k] == j
            src = src + jnp.where(hit, mrows[k] >> 3, 0)
            some = some + jnp.where(hit, 1, 0)
        piece = mig_mid[src].astype(F32)
        mig_out2[j] = jnp.where(some > 0, piece, 0.0).astype(BF16)
        return 0

    lax.fori_loop(0, 16, route_step, 0)
    keep = pltpu.make_async_copy(mig_out2.at[g], landed.at[g], loc_sem)
    keep.start()

    @pl.loop(1, 16)
    def _(i):
        mig2_copy((g + i) % 16).start()


    sent(a_send, a_s)
    sent(mig_out.at[pl.ds(0, 15)], mig_s)
    sent(sq_buf.at[pl.ds(0, 7)], sq_s)

    def agc_copy(i):
        return remote(xb.at[c, i], xb.at[c, i], agc_s, agc_r.at[i], g, partner)

    def up_part(h, yb):
        rows = jnp.concatenate(
            [xb[h, yb, k].astype(F32) for k in range(16)], axis=0
        )
        b = yb * 2 + h
        rhs = wi2_v[pl.ds(pl.multiple_of(b * BW, BW), BW), :]
        acc_v[...] += jnp.dot(rows.astype(BF16), rhs, preferred_element_type=F32)

    acc_v[...] = jnp.zeros_like(acc_v)

    taken(xb.at[c, y, pl.ds(0, 10)], ag_r.at[y])
    agc_copy(y).start()
    up_part(c, y)
    taken(xb.at[1 - c, y], agc_r.at[y])
    up_part(1 - c, y)

    def arrive_step(j, _):
        yb = (y + 4 - j) % 4
        taken(xb.at[c, yb, pl.ds(0, 10)], ag_r.at[yb])
        taken(xb.at[c, yb, pl.ds(0, 5)], fwd_r.at[yb])
        agc_copy(yb).start()
        return 0

    lax.fori_loop(1, 4, arrive_step, 0)

    def own_step(j, _):
        up_part(c, (y + 4 - j) % 4)
        return 0

    lax.fori_loop(1, 4, own_step, 0, unroll=True)

    taken(gate_buf.at[pl.ds(0, 15)], gate_r)
    gate_all = jnp.concatenate([gate_buf[k] for k in range(16)], axis=0)
    expert = g // 4
    lane_all = lax.broadcasted_iota(jnp.int32, (128, 128), 1)
    gate_col = jnp.sum(
        jnp.where(lane_all == expert, gate_all, 0.0), axis=1, keepdims=True
    )
    scale_col = gate_all[:, EXPERTS : EXPERTS + 1]

    def other_step(j, _):
        yb = (y + 4 - j) % 4
        taken(xb.at[1 - c, yb], agc_r.at[yb])
        up_part(1 - c, yb)
        return 0

    lax.fori_loop(1, 4, other_step, 0)

    gate_part = acc_v[:, 0:HID] * scale_col
    up_value = acc_v[:, HID : 2 * HID] * scale_col
    silu = gate_part / (1.0 + jnp.exp(-gate_part))
    act_v[...] = (silu * up_value * gate_col).astype(BF16)

    wd_cp.wait()

    def down(h, yb):
        b = yb * 2 + h
        cols = pl.ds(pl.multiple_of(b * BW, BW), BW)
        return jnp.dot(act_v[...], wd_v[:, cols], preferred_element_type=F32)

    def r1_copy(yb):
        return remote(r1_send.at[yb], r1_recv.at[yb], r1_s, r1_r.at[yb], g, partner)

    def block_at(j):
        return (y + jnp.where(j == 0, 2, jnp.where(j == 1, 1, jnp.where(j == 2, 3, 0)))) % 4

    def r1_step(j, _):
        yb = block_at(j)
        part = down(1 - c, yb)
        for k in range(16):
            r1_send[yb, k] = part[k * ROWS : (k + 1) * ROWS].astype(BF16)
        r1_copy(yb).start()
        return 0

    lax.fori_loop(0, 4, r1_step, 0, unroll=True)

    def r2_copy(j, yb, k):
        return remote(
            r2_send.at[yb, k], r2_recv.at[y, g], r2_s.at[j // 3], r2_r.at[y], k, yb * 2 + c
        )

    def r2_step(j, _):
        yb = block_at(j)

        @pl.when(j < 3)
        def _():
            part_v[(j + 1) % 2] = down(c, block_at(j + 1))

        taken(r1_recv.at[yb], r1_r.at[yb])
        part = part_v[j % 2]
        for k in range(16):
            both = part[k * ROWS : (k + 1) * ROWS] + r1_recv[yb, k].astype(F32)
            r2_send[yb, k] = both.astype(BF16)

        for dz, dx in FAR + NEAR:
            r2_copy(j, yb, ((z + dz) % 4) * 4 + (x + dx) % 4).start()

        @pl.when(j < 3)
        def _():
            r2_copy(j, yb, g).start()

        return 0

    part_v[0] = down(c, block_at(0))
    lax.fori_loop(0, 4, r2_step, 0)

    keep.wait()
    taken(landed.at[pl.ds(0, 15)], mig2_r)
    sent(mig_out2.at[pl.ds(0, 15)], mig2_s)
    sent(gate_buf.at[pl.ds(0, 15)], gate_s)
    sent(xb.at[0, 0, pl.ds(0, 3)], y_s)
    sent(xb.at[0, :, pl.ds(0, 10)], ag_s)
    sent(xb.at[0, 0, pl.ds(0, 5)], far_s)
    sent(xb.at[0, 0, pl.ds(0, 15)], fwd_s)
    sent(xb.at[0], agc_s)
    sent(r1_send, r1_s)

    result = hid_v[...] + r2_send[y, g].astype(F32)

    def add_from(s, first_g, count, total):
        def step(i, acc):
            return acc + r2_recv[s, (g + first_g + i) % 16].astype(F32)

        return lax.fori_loop(0, count, step, total, unroll=True)

    for j in (2, 3, 1):
        s = (y + j) % 4
        taken(r2_recv.at[s], r2_r.at[s])
        result = add_from(s, 0, 16, result)
    taken(r2_recv.at[y, pl.ds(0, 15)], r2_r.at[y])
    result = add_from(y, 1, 15, result)
    mixed[...] = result.astype(BF16)
    sent(r2_send.at[pl.ds(0, 3)], r2_s.at[0])
    sent(r2_send.at[0, pl.ds(0, 15)], r2_s.at[1])


def finish(mixed_in, landed_in, mixed_out, landed_out, sem):
    cps = [
        pltpu.make_async_copy(mixed_in, mixed_out, sem.at[0]),
        pltpu.make_async_copy(landed_in, landed_out, sem.at[1]),
    ]
    for cp in cps:
        cp.start()
    for cp in cps:
        cp.wait()


def body(
    queries,
    kv_cache,
    new_kv,
    lengths,
    residual,
    w_out,
    norm_gain,
    expert_ids,
    gate_w,
    w_inner,
    w_down,
    mig_rows,
    mig_dest,
):
    vmem = pltpu.VMEM
    dma = pltpu.SemaphoreType.DMA
    smem = pltpu.SMEM
    any_spec = pl.BlockSpec(memory_space=pl.ANY)
    vmem_spec = pl.BlockSpec(memory_space=pltpu.VMEM)
    mixed, landed = pl.pallas_call(
        kernel,
        out_shape=(
            pltpu.VMEM((ROWS, BW), BF16),
            pltpu.VMEM((16, PIECE, HD), BF16),
        ),
        in_specs=[any_spec] * 13,
        out_specs=(vmem_spec, vmem_spec),
        scratch_shapes=[
            smem((ROWS,), jnp.int32),
            smem((2, ROWS), jnp.int32),
            smem((2, ROWS), F32),
            smem((8,), jnp.int32),
            smem((8,), jnp.int32),
            vmem((HEADS, ROWS, HD), BF16),
            vmem((ROWS, 2 * SPAN, HD), BF16),
            vmem((ROWS, 2, HD), BF16),
            vmem((ROWS, BW), BF16),
            vmem((BW,), BF16),
            vmem((8, BW, BW), BF16),
            vmem((2 * D, HID), BF16),
            vmem((D, 2 * HID), BF16),
            vmem((HID, D), BF16),
            vmem((16, PIECE, HD), BF16),
            vmem((16, PIECE, HD), BF16),
            vmem((16, PIECE, HD), BF16),
            vmem((16, ROWS, 128), F32),
            vmem((7, ROWS, BW), BF16),
            vmem((8, ROWS, BW), BF16),
            vmem((ROWS, BW), F32),
            vmem((8, ROWS, 128), F32),
            vmem((2, 4, 16, ROWS, BW), BF16),
            vmem((128, HID), BF16),
            vmem((128, 2 * HID), F32),
            vmem((2, 128, BW), F32),
            vmem((4, 16, ROWS, BW), BF16),
            vmem((4, 16, ROWS, BW), BF16),
            vmem((4, 16, ROWS, BW), BF16),
            vmem((4, 16, ROWS, BW), BF16),
            dma((12,)),
            dma((8,)),
            dma,
            dma,
            dma,
            dma,
            dma,
            dma,
            dma,
            dma,
            dma,
            dma,
            dma,
            dma,
            dma((4,)),
            dma,
            dma((4,)),
            dma,
            dma,
            dma,
            dma((4,)),
            dma,
            dma((4,)),
            dma,
            dma((4,)),
            dma((2,)),
            dma((4,)),
            pltpu.SemaphoreType.REGULAR,
        ],
        compiler_params=pltpu.CompilerParams(
            collective_id=0,
            has_side_effects=True,
            vmem_limit_bytes=56 * 2**20,
        ),
        cost_estimate=pl.CostEstimate(
            flops=2 * (8 * BW * D + 256 * 2 * D * HID + 128 * HID * D),
            bytes_accessed=21 * 10**6,
            transcendentals=128 * HID,
        ),
    )(
        lengths,
        expert_ids.T,
        gate_w.T,
        mig_rows,
        mig_dest,
        queries.transpose(1, 0, 2),
        kv_cache.reshape(ROWS, 2 * SPAN, HD),
        new_kv.reshape(ROWS, 2, HD),
        residual,
        norm_gain,
        w_out,
        w_inner,
        w_down,
    )
    mixed, landed = pl.pallas_call(
        finish,
        out_shape=(
            jax.ShapeDtypeStruct((ROWS, BW), BF16),
            jax.ShapeDtypeStruct((16, PIECE, HD), BF16),
        ),
        in_specs=[vmem_spec] * 2,
        out_specs=(any_spec, any_spec),
        scratch_shapes=[dma((2,))],
        compiler_params=pltpu.CompilerParams(vmem_limit_bytes=56 * 2**20),
    )(
        pltpu.with_memory_space_constraint(mixed, pltpu.VMEM),
        pltpu.with_memory_space_constraint(landed, pltpu.VMEM),
    )
    return mixed, landed.reshape(1, 2, 1, SPAN, HD)


def solution(mesh):
    in_specs = (
        P("grp", "tp", None),
        P("grp", None, "tp", None, None),
        P("grp", None, "tp", None),
        P("grp"),
        P("grp", "tp"),
        P("tp", None),
        P("tp"),
        P("grp", None),
        P("grp", None),
        P(None, None, ("grp", "tp")),
        P(("grp", "tp"), None),
        P(),
        P(),
    )
    out_specs = (P("grp", "tp"), P("grp", None, "tp", None, None))
    return jax.shard_map(body, mesh=mesh, in_specs=in_specs, out_specs=out_specs, check_vma=False)
```
